256 devices in a mesh: ctx: 64 (over y, z, core), head: 4 (over x).
Axes of the slice: x: 4, y: 4, z: 8, core: 2. Of those that a mesh axis runs over, the one named last changes fastest.
Arguments:
- tokens: bfloat16 [32768, 5120], P('ctx', 'head'), may hold values from -48 to 48
- w_query: bfloat16 [5120, 2560], P(None, 'head'), may hold values from -0.078125 to 0.078125
- key_value_weight: bfloat16 [5120, 2, 512], P(None, None, 'head'), may hold values from -0.078125 to 0.078125
- bias_query: float32 [2560], P('head'), may hold values from -3 to 3
- key_value_bias: float32 [2, 512], P(None, 'head'), may hold values from -3 to 3
- destination: int32 [4096], replicated, may hold values from 0 to 4095, as said below
- doc_ids: int32 [4096], replicated, may hold values from 0 to 127, never falling along the last dimension, each value on 1 to 384 neighbouring positions
Outputs:
- attended: bfloat16 [32768, 2560], P('ctx', 'head')
The draws below stay inside these ranges and needn't reach their ends.
Inputs may be any that keep to these rules, and one draw needn't show every extreme that they name: A permutation of the 4096 blocks: old block b, held by ctx index b // 64, goes to ctx index destination[b] // 64. The blocks of each old holder go to exactly 64 new holders, 1 to each. `doc_ids`: Non-decreasing; each document covers 1 to 384 consecutive blocks.
All inputs are finite; a program needn't handle non-finite values.
Results may differ from the reference program's by a relative error of at most 0.012.
The reference program's roundings to bfloat16 on the way count: a program that leaves them out, or rounds other values in their place, can miss the bound.
Values may be sent and summed in bfloat16 or wider, within the bound.
A program may use at most 64 MiB of HBM per device.

```python
import math
import jax
import jax.numpy as jnp
import numpy as np
from jax import lax

MODEL_DIM = 5120
QUERY_HEADS = 20
KEY_VALUE_HEADS = 4
HEAD_SIZE = 128
BLOCK = 8
BLK_DEV = 64
HOPS = 6
TOKENS_PER_SHARD = 512
NB = 4096
TOKENS = 32768
TARGETS = 64
CAP = 1
MAXDOC = 384
NDOCS = 128
N_CTX = 64


def draw_tokens(key, part):
    key = jax.random.fold_in(key, 5)
    key_base = jax.random.fold_in(key, 0)
    values = jax.random.normal(key_base, (TOKENS, MODEL_DIM), jnp.float32)
    return jnp.clip(values, -6.0, 6.0).astype(jnp.bfloat16)


def draw_destination(key, part):
    key = jax.random.fold_in(key, 11)
    key_old, key_new, key_slots, key_within = jax.random.split(key, 4)
    shuffle_old = jax.random.permutation(key_old, N_CTX).astype(jnp.int32)
    shuffle_new = jax.random.permutation(key_new, N_CTX).astype(jnp.int32)
    allowed = (shuffle_old[:, None] + shuffle_new[None, :]) % N_CTX < TARGETS
    indices = jnp.arange(N_CTX, dtype=jnp.int32)
    sort_keys = jnp.where(allowed, indices[None, :], indices[None, :] + N_CTX)
    target_table = jnp.argsort(sort_keys, axis=1)[:, :TARGETS].astype(jnp.int32)
    base_slots = jnp.tile(jnp.arange(BLK_DEV, dtype=jnp.int32)[None, :], (N_CTX, 1))
    slot_order = jax.random.permutation(key_slots, base_slots, axis=1, independent=True)
    target = jnp.take_along_axis(target_table, slot_order // CAP, axis=1)
    copy_index = slot_order % CAP
    sender_rank = jnp.cumsum(allowed.astype(jnp.int32), axis=0) - 1
    rank_here = sender_rank[indices[:, None], target]
    within = jax.random.permutation(key_within, base_slots, axis=1, independent=True)
    new_slot = within[target, rank_here * CAP + copy_index]
    return (target * BLK_DEV + new_slot).reshape(NB).astype(jnp.int32)


def steps_of(rng, dims, cuts, smallest, top_value):
    level, own = 1.0, jax.random.fold_in(rng, 6)
    for dim, blocks in cuts:
        steps = jnp.exp(jax.random.uniform(jax.random.fold_in(own, dim), (blocks,), jnp.float32, smallest / len(cuts), top_value / len(cuts)))
        level = level * jnp.repeat(steps, dims[dim] // blocks).reshape([-1 if axis == dim else 1 for axis in range(len(dims))])
    return level


def split_up(count, total, bound, skew):
    loads = [(1 << 20) // math.isqrt(rank ** skew) + 1 for rank in range(2, count + 1)]
    rest, counts = total - bound - (count - 1), [1] * (count - 1)
    while rest > 0:
        candidates = [i for i in range(count - 1) if counts[i] < bound]
        mass, left = sum([loads[i] for i in candidates]), rest
        for i in candidates:
            extra = min(bound - counts[i], max(1, left * loads[i] // mass), rest)
            counts[i] = counts[i] + extra
            rest = rest - extra
    return np.array([bound] + counts)


def uneven_parts(key, count, total, most, slope):
    if count == 2:
        one = jax.random.randint(key, (), max(1, total - most), min(most, total - 1) + 1)
        return jnp.stack([one, total - one])
    lengths = jnp.asarray(split_up(count, total, most, slope), jnp.int32)
    pairs = (count - 1) // 2
    donor, sink = lengths[1:1 + 2 * pairs:2], lengths[2:2 + 2 * pairs:2]
    margin = jnp.minimum(donor - 1, most - sink)
    passed = jax.random.randint(jax.random.fold_in(key, 1), (pairs,), 0, 1 << 20) % (margin + 1)
    lengths = lengths.at[1:1 + 2 * pairs:2].set(donor - passed).at[2:2 + 2 * pairs:2].set(sink + passed)
    return lengths[jax.random.permutation(jax.random.fold_in(key, 2), count)]


def gaussian(own_key, extent, scale, reach, cuts=(), kind=jnp.bfloat16):
    result = jax.random.normal(own_key, extent, jnp.float32) * scale
    if len(cuts) > 0:
        result = steps_of(own_key, extent, cuts, -0.22, 0.18) * result
    return jnp.clip(result, min=-reach, max=reach).astype(kind)


def setup_inputs(seed: int = 0) -> dict:
    splits = jax.random.split(jax.random.key(seed), 8)
    return {
        "tokens": draw_tokens(jax.random.fold_in(splits[7], 71), 0),
        "w_query": gaussian(splits[1], (MODEL_DIM, QUERY_HEADS * HEAD_SIZE), MODEL_DIM ** -0.5, 0.078125, ((1, 4),)),
        "key_value_weight": gaussian(splits[2], (MODEL_DIM, 2, KEY_VALUE_HEADS * HEAD_SIZE), MODEL_DIM ** -0.5, 0.078125, ((2, 4),)),
        "bias_query": gaussian(splits[3], (QUERY_HEADS * HEAD_SIZE,), 0.5, 3.0, ((0, 4),), jnp.float32),
        "key_value_bias": gaussian(splits[4], (2, KEY_VALUE_HEADS * HEAD_SIZE), 0.5, 3.0, ((1, 4),), jnp.float32),
        "destination": draw_destination(jax.random.fold_in(splits[7], 71), 0),
        "doc_ids": jnp.searchsorted(jnp.cumsum(uneven_parts(splits[6], NDOCS, NB, MAXDOC, 2)), jnp.arange(NB), side="right").astype(jnp.int32),
    }


def reference(tokens, w_query, key_value_weight, bias_query, key_value_bias, destination, doc_ids):
    block_rows = tokens.reshape(NB, BLOCK, MODEL_DIM)
    reordered_rows = jnp.zeros_like(block_rows).at[destination].set(block_rows).reshape(TOKENS, MODEL_DIM)
    query_matrix = (jnp.dot(reordered_rows, w_query, preferred_element_type=jnp.float32) + bias_query).astype(jnp.bfloat16)
    projected_rows = jnp.dot(reordered_rows, key_value_weight.reshape(MODEL_DIM, 2 * KEY_VALUE_HEADS * HEAD_SIZE), preferred_element_type=jnp.float32)
    projected_rows = (projected_rows + key_value_bias.reshape(2 * KEY_VALUE_HEADS * HEAD_SIZE)).astype(jnp.bfloat16)
    key_head_split = projected_rows[:, :KEY_VALUE_HEADS * HEAD_SIZE]
    value_head_split = projected_rows[:, KEY_VALUE_HEADS * HEAD_SIZE:]
    border_extent = HOPS * TOKENS_PER_SHARD
    visible_span = (HOPS + 1) * TOKENS_PER_SHARD
    key_padding = jnp.concatenate([jnp.zeros((border_extent, KEY_VALUE_HEADS * HEAD_SIZE), key_head_split.dtype), key_head_split], axis=0)
    value_padding = jnp.concatenate([jnp.zeros((border_extent, KEY_VALUE_HEADS * HEAD_SIZE), value_head_split.dtype), value_head_split], axis=0)
    doc_tokens = jnp.repeat(doc_ids, BLOCK).astype(jnp.int32)
    doc_pad = jnp.concatenate([jnp.full((border_extent,), -1, jnp.int32), doc_tokens], axis=0)
    query_group_width = QUERY_HEADS // KEY_VALUE_HEADS
    score_scale = 1.0 / math.sqrt(HEAD_SIZE)

    def one_shard(shard):
        start_offset = (shard * TOKENS_PER_SHARD).astype(jnp.int32)
        query_row_block = lax.dynamic_slice_in_dim(query_matrix, start_offset, TOKENS_PER_SHARD, 0).reshape(TOKENS_PER_SHARD, KEY_VALUE_HEADS, query_group_width, HEAD_SIZE).astype(jnp.float32)
        key_row_block = lax.dynamic_slice_in_dim(key_padding, start_offset, visible_span, 0).reshape(visible_span, KEY_VALUE_HEADS, HEAD_SIZE).astype(jnp.float32)
        value_row_block = lax.dynamic_slice_in_dim(value_padding, start_offset, visible_span, 0).reshape(visible_span, KEY_VALUE_HEADS, HEAD_SIZE).astype(jnp.float32)
        q_docs = lax.dynamic_slice_in_dim(doc_tokens, start_offset, TOKENS_PER_SHARD, 0)
        k_docs = lax.dynamic_slice_in_dim(doc_pad, start_offset, visible_span, 0)
        q_pos = start_offset + jnp.arange(TOKENS_PER_SHARD, dtype=jnp.int32)
        k_pos = start_offset - border_extent + jnp.arange(visible_span, dtype=jnp.int32)
        visible = (q_docs[:, None] == k_docs[None, :]) & (k_pos[None, :] <= q_pos[:, None])
        scores = jnp.einsum('tkgd,skd->kgts', query_row_block, key_row_block) * score_scale
        masked = jnp.where(visible[None, None], scores, -1e+30)
        highest = lax.optimization_barrier(jnp.max(masked, axis=-1, keepdims=True))
        weights = jnp.where(visible[None, None], jnp.exp(masked - highest), 0.0)
        denominator = lax.optimization_barrier(jnp.sum(weights, axis=-1))
        rounded = lax.optimization_barrier(weights.astype(jnp.bfloat16)).astype(jnp.float32)
        mixed = jnp.einsum('kgts,skd->tkgd', rounded, value_row_block)
        mixed = mixed / jnp.transpose(denominator, (2, 0, 1))[..., None]
        return mixed.reshape(TOKENS_PER_SHARD, QUERY_HEADS * HEAD_SIZE).astype(jnp.bfloat16)
    attended = lax.map(one_shard, jnp.arange(N_CTX, dtype=jnp.int32))
    return attended.reshape(TOKENS, QUERY_HEADS * HEAD_SIZE)
```

```python
import functools
import math

import jax
import jax.numpy as jnp
from jax import lax
from jax.experimental import pallas as pl
from jax.experimental.pallas import tpu as pltpu
from jax.sharding import PartitionSpec as P

MESH = pl.DeviceIdType.MESH
HEAD_SIZE = 128
HEADS = 5
BLOCK = 8
Y, Z, C, X = 4, 8, 2, 4
N = Y * Z * C
G = 4
PER = N // G
ROWS = PER * BLOCK
SHARD = N * BLOCK
HALF = 640
DEPTH = 2 * HALF
QW = HEADS * HEAD_SIZE
DISTANCES = (0, 2, 4, 6, 1, 3, 5)
NBUF = len(DISTANCES)
KEYS = NBUF * ROWS
NEG = -1e30
SCALE = 1.0 / math.sqrt(HEAD_SIZE) * math.log2(math.e)


def offset_of(slot):
    g, r = slot // PER, slot % PER
    dz, dc = r // C, r % C
    return (g + dz) % Y, dz, dc


def moved(ctx, offset, sign):
    dy, dz, dc = offset
    y, z, c = ctx // (Z * C), (ctx // C) % Z, ctx % C
    y = (y + sign * dy + Y) % Y
    z = (z + sign * dz + Z) % Z
    c = (c + sign * dc + C) % C
    return (y * Z + z) * C + c


def kernel(pick, inv, kpos, qlo, qhi, bq, bkv, tokens, wq_hbm, wkv_hbm, out,
           tok, send, xg, wq, wraw, wkv, acc, qs, kv, pb, m_ref, l_ref, o_ref, on, stage,
           local_sem, a2a_send, a2a_recv, xs_send, x_recv, rl_send, rl_recv,
           kv_send, kv_recv, pb_send, pb_recv):
    me = lax.axis_index("ctx")
    x = lax.axis_index("head")
    core = lax.rem(me, C)
    right, left = lax.rem(x + 1, X), lax.rem(x + X - 1, X)
    onward = lax.rem(me + C, N)
    partner = me + 1 - 2 * core

    load_tok = pltpu.make_async_copy(tokens, tok, local_sem.at[0])
    load_wq = pltpu.make_async_copy(wq_hbm, wq, local_sem.at[1])
    load_wkv = pltpu.make_async_copy(wkv_hbm, wraw, local_sem.at[2])
    load_tok.start()
    load_wkv.start()
    load_wq.start()

    barrier = pltpu.get_barrier_semaphore()

    @pl.loop(1, N)
    def _(s):
        pl.semaphore_signal(barrier, inc=1, device_id=(moved(me, offset_of(s), 1), x), device_id_type=MESH)

    pl.semaphore_signal(barrier, inc=1, device_id=(me, right), device_id_type=MESH)
    pl.semaphore_signal(barrier, inc=1, device_id=(me, left), device_id_type=MESH)

    load_tok.wait()

    @pl.loop(0, N)
    def _(s):
        rows = tok[pick[s]].astype(jnp.float32)
        both = jnp.concatenate([rows[:, :HALF], rows[:, HALF:]], axis=0)
        send[s] = both.astype(jnp.bfloat16)

    pl.semaphore_wait(barrier, N + 1)

    def a2a(s, g):
        return pltpu.make_async_remote_copy(
            src_ref=send.at[s], dst_ref=xg.at[0, s], send_sem=a2a_send, recv_sem=a2a_recv.at[g],
            device_id=(moved(me, offset_of(s), 1), x), device_id_type=MESH)

    own = pltpu.make_async_copy(send.at[0], xg.at[0, 0], a2a_recv.at[0])
    own.start()

    @pl.loop(1, N)
    def _(s):
        a2a(s, s // PER).start()

    def group(g):
        return pl.ds(g * PER, PER)

    def x_send(g, side):
        return pltpu.make_async_remote_copy(
            src_ref=xg.at[0, group(g)], dst_ref=xg.at[1 + side, group(g)],
            send_sem=xs_send.at[side, g], recv_sem=x_recv.at[side, g],
            device_id=(me, right if side == 0 else left), device_id_type=MESH)

    def relay(g, side):
        half = pl.ds(g * PER + side * (PER // 2), PER // 2)
        return pltpu.make_async_remote_copy(
            src_ref=xg.at[1 + side, half], dst_ref=xg.at[3, half],
            send_sem=rl_send.at[side, g], recv_sem=rl_recv.at[side, g],
            device_id=(me, right if side == 0 else left), device_id_type=MESH)

    def kv_copy(g, h):
        return pltpu.make_async_remote_copy(
            src_ref=kv.at[h, g], dst_ref=kv.at[h + 1, g],
            send_sem=kv_send.at[h, g], recv_sem=kv_recv.at[h, g],
            device_id=(onward, x), device_id_type=MESH)

    def pb_copy(g, i):
        return pltpu.make_async_remote_copy(
            src_ref=kv.at[i + core, g], dst_ref=pb.at[i, g],
            send_sem=pb_send.at[i, g], recv_sem=pb_recv.at[i, g],
            device_id=(partner, x), device_id_type=MESH)

    def group_ready(g):
        pltpu.make_async_copy(xg.at[0, group(g)], xg.at[0, group(g)], a2a_recv.at[g]).wait()
        x_send(g, 0).start()
        x_send(g, 1).start()

    def chain(g, h):
        kv_copy(g, h - 1).wait_recv()
        if h < 3:
            kv_copy(g, h).start()
        pb_copy(g, h - 1).start()

    def chain_end(g):
        for i in range(3):
            pb_copy(g, i).wait_recv()

    load_wkv.wait()

    @pl.loop(0, 20)
    def _(t):
        raw = wraw[pl.ds(t * 512, 512), :].astype(jnp.float32)
        stage[...] = raw
        rows = pl.ds(t * 256, 256)
        wkv[rows, :HEAD_SIZE] = stage[pl.ds(0, 256, 2), :].astype(jnp.bfloat16)
        wkv[rows, HEAD_SIZE:] = stage[pl.ds(1, 256, 2), :].astype(jnp.bfloat16)

    m_ref[...] = jnp.full_like(m_ref, NEG)
    l_ref[...] = jnp.zeros_like(l_ref)
    o_ref[...] = jnp.zeros_like(o_ref)

    def project_part(g, part, peer):
        piece = xg[part, group(g)].astype(jnp.float32)
        lhs = jnp.concatenate(
            [piece[:, :BLOCK].reshape(ROWS, HALF), piece[:, BLOCK:].reshape(ROWS, HALF)], axis=1
        ).astype(jnp.bfloat16)
        depth = pl.ds(pl.multiple_of(peer * DEPTH, DEPTH), DEPTH)
        acc[:, :QW] += jnp.dot(lhs, wq[depth, :], preferred_element_type=jnp.float32)
        acc[:, QW:] += jnp.dot(lhs, wkv[depth, :], preferred_element_type=jnp.float32)

    def project(g):
        acc[...] = jnp.concatenate(
            [jnp.broadcast_to(bq[...], (ROWS, QW)),
             jnp.broadcast_to(bkv[0:1, :], (ROWS, HEAD_SIZE)),
             jnp.broadcast_to(bkv[1:2, :], (ROWS, HEAD_SIZE))], axis=1)

        @pl.loop(0, 4)
        def _(part):
            @pl.when(part == 3)
            def _():
                relay(g, 0).wait_recv()
                relay(g, 1).wait_recv()

            shift = jnp.where(part == 3, 2, jnp.where(part == 1, X - 1, jnp.where(part == 2, 1, 0)))
            project_part(g, part, lax.rem(x + shift, X))

        for h in range(HEADS):
            qs[g, pl.ds(h * ROWS, ROWS), :] = acc[:, h * HEAD_SIZE:(h + 1) * HEAD_SIZE].astype(jnp.bfloat16)
        kv[0, g] = acc[:, QW:].astype(jnp.bfloat16)
        kv_copy(g, 0).start()

    def attend(i, j):
        keys = jnp.concatenate(
            [kv[h, j][:, :HEAD_SIZE] for h in range(4)] + [pb[h, j][:, :HEAD_SIZE] for h in range(3)], axis=0)
        values = jnp.concatenate(
            [kv[h, j][:, HEAD_SIZE:] for h in range(4)] + [pb[h, j][:, HEAD_SIZE:] for h in range(3)], axis=0)
        place = kpos[j]
        bias = jnp.where((place <= qhi[i]) & (place >= qlo[i]), 0.0, NEG)
        s = lax.dot_general(qs[i], keys, (((1,), (1,)), ((), ())), preferred_element_type=jnp.float32)
        s = (s.reshape(HEADS, ROWS, KEYS) + bias[None]).reshape(HEADS * ROWS, KEYS)
        m_old = m_ref[i]
        m_new = jnp.maximum(m_old, jnp.max(s, axis=1, keepdims=True))
        p = jnp.exp2((s - m_new[:, :1]) * SCALE)
        alpha = jnp.exp2((m_old - m_new) * SCALE)
        l_ref[i] = l_ref[i] * alpha + jnp.sum(p, axis=1, keepdims=True)
        o_ref[i] = o_ref[i] * alpha + jnp.dot(p.astype(jnp.bfloat16), values, preferred_element_type=jnp.float32)
        m_ref[i] = m_new

    group_ready(0)
    load_wq.wait()

    @pl.loop(0, G + 2)
    def _(step):
        @pl.when(step >= 2)
        def _():
            j = step - 2
            chain_end(j)
            rows_there = jnp.minimum(step, G)
            older = jnp.where(step <= G, j, 0)

            @pl.loop(0, rows_there + older)
            def _(t):
                i = jnp.where(t < rows_there, t, rows_there - 1)
                jj = jnp.where(t < rows_there, j, t - rows_there)
                attend(i, jj)

        @pl.when(step < G)
        def _():
            x_send(step, 0).wait_recv()
            relay(step, 0).start()
            x_send(step, 1).wait_recv()
            relay(step, 1).start()

        @pl.when(step + 1 < G)
        def _():
            group_ready(step + 1)

        @pl.when((step >= 1) & (step <= G))
        def _():
            chain(step - 1, 1)

        @pl.when(step < G)
        def _():
            project(step)

        @pl.when((step >= 1) & (step <= G))
        def _():
            chain(step - 1, 2)
            chain(step - 1, 3)

    @pl.loop(0, G)
    def _(g):
        for h in range(HEADS):
            rows = pl.ds(h * ROWS, ROWS)
            part = o_ref[g, rows, :] / l_ref[g, rows, :]
            on[pl.ds(h * N + g * PER, PER)] = part.reshape(PER, BLOCK, HEAD_SIZE)

    @pl.loop(0, N // 2)
    def _(t):
        first, second = inv[2 * t], inv[2 * t + 1]
        rows = pl.ds(t * 2 * BLOCK, 2 * BLOCK)
        for h in range(HEADS):
            pair = jnp.concatenate([on[h * N + first], on[h * N + second]], axis=0)
            out[rows, h * HEAD_SIZE:(h + 1) * HEAD_SIZE] = pair.astype(jnp.bfloat16)

    pltpu.make_async_copy(send.at[pl.ds(1, N - 1)], send.at[pl.ds(1, N - 1)], a2a_send).wait()

    @pl.loop(0, G)
    def _(g):
        for side in range(2):
            x_send(g, side).wait_send()
            relay(g, side).wait_send()
        for h in range(3):
            kv_copy(g, h).wait_send()
            pb_copy(g, h).wait_send()


def per_device(tokens, w_query, key_value_weight, bias_query, key_value_bias, destination, doc_ids):
    me = lax.axis_index("ctx")
    slots = jnp.arange(N, dtype=jnp.int32)
    table = destination.reshape(N, N)
    target = moved(me, offset_of(slots), 1)
    mine = lax.dynamic_slice_in_dim(table, me, 1)[0]
    pick = jnp.sum(jnp.where((mine // N)[None, :] == target[:, None], slots[None, :], 0), axis=1)
    shards = me - jnp.array(DISTANCES, jnp.int32)
    wrapped = (shards + N) % N
    place = jnp.sum(jnp.where((table // N)[None] == wrapped[:, None, None], (table % N)[None], 0), axis=2)
    senders = jnp.stack(
        [moved(wrapped[d], offset_of(slots), -1) for d in range(NBUF)])
    in_slot = jnp.sum(jnp.where(senders[:, :, None] == slots[None, None, :], place[:, None, :], 0), axis=2)
    inv = jnp.sum(jnp.where(in_slot[0][None, :] == slots[:, None], slots[None, :], 0), axis=1)
    lanes = jnp.arange(BLOCK, dtype=jnp.int32)
    token_at = shards[:, None, None] * SHARD + in_slot[:, :, None] * BLOCK + lanes
    kpos = token_at.reshape(NBUF, G, ROWS).transpose(1, 0, 2).reshape(G, 1, KEYS)
    qhi = token_at[0].reshape(G, ROWS, 1)
    docs = lax.dynamic_slice_in_dim(doc_ids, me * N, N)
    starts = jnp.sum((doc_ids[None, :] < docs[:, None]).astype(jnp.int32), axis=1) * BLOCK
    start_in_slot = jnp.sum(jnp.where(in_slot[0][:, None] == slots[None, :], starts[None, :], 0), axis=1)
    qlo = jnp.broadcast_to(start_in_slot[:, None], (N, BLOCK)).reshape(G, ROWS, 1)

    vmem, smem, hbm = (pl.BlockSpec(memory_space=s) for s in (pltpu.VMEM, pltpu.SMEM, pl.ANY))
    bf16, f32 = jnp.bfloat16, jnp.float32
    dma = pltpu.SemaphoreType.DMA
    return pl.pallas_call(
        kernel,
        out_shape=jax.ShapeDtypeStruct((SHARD, QW), bf16),
        in_specs=[smem, smem, vmem, vmem, vmem, vmem, vmem, hbm, hbm, hbm],
        out_specs=vmem,
        scratch_shapes=[
            pltpu.VMEM((N, BLOCK, DEPTH), bf16),
            pltpu.VMEM((N, 2 * BLOCK, HALF), bf16),
            pltpu.VMEM((X, N, 2 * BLOCK, HALF), bf16),
            pltpu.VMEM((X * DEPTH, QW), bf16),
            pltpu.VMEM((2 * X * DEPTH, HEAD_SIZE), bf16),
            pltpu.VMEM((X * DEPTH, 2 * HEAD_SIZE), bf16),
            pltpu.VMEM((ROWS, QW + 2 * HEAD_SIZE), f32),
            pltpu.VMEM((G, HEADS * ROWS, HEAD_SIZE), bf16),
            pltpu.VMEM((4, G, ROWS, 2 * HEAD_SIZE), bf16),
            pltpu.VMEM((3, G, ROWS, 2 * HEAD_SIZE), bf16),
            pltpu.VMEM((G, HEADS * ROWS, HEAD_SIZE), f32),
            pltpu.VMEM((G, HEADS * ROWS, HEAD_SIZE), f32),
            pltpu.VMEM((G, HEADS * ROWS, HEAD_SIZE), f32),
            pltpu.VMEM((HEADS * N, BLOCK, HEAD_SIZE), f32),
            pltpu.VMEM((512, HEAD_SIZE), f32),
            dma((3,)), dma, dma((G,)),
            dma((2, G)), dma((2, G)), dma((2, G)), dma((2, G)),
            dma((3, G)), dma((3, G)), dma((3, G)), dma((3, G)),
        ],
        compiler_params=pltpu.CompilerParams(
            collective_id=0, has_side_effects=True, vmem_limit_bytes=56 * 1024 * 1024),
    )(pick, inv, kpos, qlo, qhi, bias_query.reshape(1, QW), key_value_bias,
      tokens.reshape(N, BLOCK, DEPTH), w_query, key_value_weight.reshape(2 * X * DEPTH, HEAD_SIZE))


def solution(mesh):
    placed = (
        P("ctx", "head"),
        P(None, "head"),
        P(None, None, "head"),
        P("head"),
        P(None, "head"),
        P(),
        P(),
    )
    return jax.shard_map(
        per_device, mesh=mesh, in_specs=placed, out_specs=P("ctx", "head"), check_vma=False
    )
```

```python
import functools
import math

import jax
import jax.numpy as jnp
from jax import lax
from jax.experimental import pallas as pl
from jax.experimental.pallas import tpu as pltpu
from jax.sharding import PartitionSpec as P

MESH = pl.DeviceIdType.MESH
HEAD_SIZE = 128
HEADS = 5
BLOCK = 8
Y, Z, C, X = 4, 8, 2, 4
N = Y * Z * C
G = 4
PER = N // G
ROWS = PER * BLOCK
SHARD = N * BLOCK
HALF = 640
DEPTH = 2 * HALF
QW = HEADS * HEAD_SIZE
DISTANCES = (0, 2, 4, 6, 1, 3, 5)
NBUF = len(DISTANCES)
KEYS = NBUF * ROWS
NEG = -1e30
SCALE = 1.0 / math.sqrt(HEAD_SIZE) * math.log2(math.e)


def slot_parts(slot):
    dz, dc = (slot >> 1) & (Z - 1), slot & 1
    return ((slot >> 4) + dz) & (Y - 1), dz, dc


def sender_of(ctx, slot):
    dy, dz, dc = slot_parts(slot)
    return ((((ctx >> 4) - dy) & (Y - 1)) << 4) + ((((ctx >> 1) - dz) & (Z - 1)) << 1) + ((ctx - dc) & 1)


def target_of(ctx, slot):
    dy, dz, dc = slot_parts(slot)
    return ((((ctx >> 4) + dy) & (Y - 1)) << 4) + ((((ctx >> 1) + dz) & (Z - 1)) << 1) + ((ctx + dc) & 1)


def iota(shape, dim):
    return lax.broadcasted_iota(jnp.int32, shape, dim)


def kernel(table, docs, bq, bkv, tokens, wq_hbm, wkv_hbm, out,
           tok, send, xg, wq, wraw, wkv, acc, qs, kv, pb, m_ref, l_ref, o_ref, on, stage,
           kpos, qlo, qhi, qplace,
           local_sem, a2a_send, a2a_recv, xs_send, x_recv, rl_send, rl_recv,
           kv_send, kv_recv, pb_send, pb_recv):
    me = lax.axis_index("ctx")
    x = lax.axis_index("head")
    core = lax.rem(me, C)
    my_y, my_z = lax.div(me, Z * C), lax.rem(lax.div(me, C), Z)
    right, left = lax.rem(x + 1, X), lax.rem(x + X - 1, X)
    onward = lax.rem(me + C, N)
    partner = me + 1 - 2 * core

    load_tok = pltpu.make_async_copy(tokens, tok, local_sem.at[0])
    load_wq = pltpu.make_async_copy(wq_hbm, wq, local_sem.at[1])
    load_wkv = pltpu.make_async_copy(wkv_hbm, wraw, local_sem.at[2])
    load_tok.start()
    load_wkv.start()
    load_wq.start()

    barrier = pltpu.get_barrier_semaphore()

    def chip_at(u):
        g, dz = lax.div(u, Z), lax.rem(u, Z)
        return (lax.rem(my_y + lax.rem(g + dz, Y), Y) * Z + lax.rem(my_z + dz, Z)) * C

    def cores_at(u):
        chip = chip_at(u)
        return (2 * u, chip + core), (2 * u + 1, chip + 1 - core)

    pl.semaphore_signal(barrier, inc=1, device_id=(partner, x), device_id_type=MESH)

    @pl.loop(1, N // 2)
    def _(u):
        for _, target in cores_at(u):
            pl.semaphore_signal(barrier, inc=1, device_id=(target, x), device_id_type=MESH)

    pl.semaphore_signal(barrier, inc=1, device_id=(me, right), device_id_type=MESH)
    pl.semaphore_signal(barrier, inc=1, device_id=(me, left), device_id_type=MESH)

    shift = (me & 1) * N
    mine = table[pl.ds(lax.div(me, 2), 1), :]
    spread = jnp.where(iota((128, SHARD), 0) == shift + (iota((128, SHARD), 1) >> 3), 1.0, 0.0).astype(jnp.bfloat16)
    owners = jnp.broadcast_to((mine >> 6).astype(jnp.float32).astype(jnp.bfloat16), (8, 128))
    owner_of = jnp.dot(owners, spread, preferred_element_type=jnp.float32)[0:1].astype(jnp.int32)
    load_tok.wait()
    for g in range(G):
        row = iota((ROWS, 1), 0)
        target = target_of(me, (row >> 3) + g * PER)
        pick = (owner_of == target) & ((iota((1, SHARD), 1) & 7) == (row & 7))
        picked = jnp.dot(jnp.where(pick, 1.0, 0.0).astype(jnp.bfloat16), tok[...], preferred_element_type=jnp.float32)
        halves = [picked[:, h * HALF:(h + 1) * HALF].reshape(PER, BLOCK, HALF) for h in range(2)]
        send[pl.ds(g * PER, PER)] = jnp.concatenate(halves, axis=1).astype(jnp.bfloat16)

    pl.semaphore_wait(barrier, N + 1)

    def a2a(s, target):
        return pltpu.make_async_remote_copy(
            src_ref=send.at[s], dst_ref=xg.at[0, s], send_sem=a2a_send, recv_sem=a2a_recv.at[lax.div(s, PER)],
            device_id=(target, x), device_id_type=MESH)

    own = pltpu.make_async_copy(send.at[0], xg.at[0, 0], a2a_recv.at[0])
    own.start()
    a2a(1, partner).start()

    @pl.loop(1, N // 2)
    def _(u):
        for s, target in cores_at(u):
            a2a(s, target).start()

    def group(g):
        return pl.ds(g * PER, PER)

    def x_send(g, side):
        return pltpu.make_async_remote_copy(
            src_ref=xg.at[0, group(g)], dst_ref=xg.at[1 + side, group(g)],
            send_sem=xs_send.at[side, g], recv_sem=x_recv.at[side, g],
            device_id=(me, right if side == 0 else left), device_id_type=MESH)

    def relay(g, side):
        half = pl.ds(g * PER + side * (PER // 2), PER // 2)
        return pltpu.make_async_remote_copy(
            src_ref=xg.at[1 + side, half], dst_ref=xg.at[3, half],
            send_sem=rl_send.at[side, g], recv_sem=rl_recv.at[side, g],
            device_id=(me, right if side == 0 else left), device_id_type=MESH)

    def kv_copy(g, h):
        return pltpu.make_async_remote_copy(
            src_ref=kv.at[h, g], dst_ref=kv.at[h + 1, g],
            send_sem=kv_send.at[h, g], recv_sem=kv_recv.at[h, g],
            device_id=(onward, x), device_id_type=MESH)

    def pb_copy(g, i):
        return pltpu.make_async_remote_copy(
            src_ref=kv.at[i + core, g], dst_ref=pb.at[i, g],
            send_sem=pb_send.at[i, g], recv_sem=pb_recv.at[i, g],
            device_id=(partner, x), device_id_type=MESH)

    def group_ready(g):
        pltpu.make_async_copy(xg.at[0, group(g)], xg.at[0, group(g)], a2a_recv.at[g]).wait()
        x_send(g, 0).start()
        x_send(g, 1).start()

    def chain(g, h):
        kv_copy(g, h - 1).wait_recv()
        if h < 3:
            kv_copy(g, h).start()
        pb_copy(g, h - 1).start()

    def chain_end(g):
        for i in range(3):
            pb_copy(g, i).wait_recv()

    load_wkv.wait()

    @pl.loop(0, 20)
    def _(t):
        raw = wraw[pl.ds(t * 512, 512), :].astype(jnp.float32)
        stage[...] = raw
        rows = pl.ds(t * 256, 256)
        wkv[rows, :HEAD_SIZE] = stage[pl.ds(0, 256, 2), :].astype(jnp.bfloat16)
        wkv[rows, HEAD_SIZE:] = stage[pl.ds(1, 256, 2), :].astype(jnp.bfloat16)

    entry = table[...]
    entry_place = (entry & (N - 1)).astype(jnp.float32)
    lane = iota((1, 128), 1)
    lane_slot = iota((1, SHARD), 1) >> 3
    lane_token = (iota((1, SHARD), 1) & 7).astype(jnp.float32)
    pair = iota((N // 2, 1), 0)
    for buf, distance in enumerate(DISTANCES):
        shard = me - distance
        wrapped = shard & (N - 1)
        found = jnp.where((entry >> 6) == wrapped, entry_place, 0.0)
        even = jnp.sum(jnp.where(lane < N, found, 0.0), axis=1, keepdims=True)
        odd = jnp.sum(jnp.where(lane < N, 0.0, found), axis=1, keepdims=True)
        sender = sender_of(wrapped, lane_slot)
        hit = (sender >> 1) == pair
        place = jnp.sum(jnp.where(hit, jnp.where((sender & 1) == 0, even, odd), 0.0), axis=0, keepdims=True)
        row = (shard * SHARD).astype(jnp.float32) + place * BLOCK + lane_token
        for g in range(G):
            kpos[g, 0:1, buf * ROWS:(buf + 1) * ROWS] = row[:, g * ROWS:(g + 1) * ROWS]
        if buf == 0:
            mate = (lane >> 1) == pair
            place_row = jnp.sum(jnp.where(mate, jnp.where((lane & 1) == 0, even, odd), 0.0), axis=0, keepdims=True)
            row_index = iota((SHARD, 1), 0)
            mine_from = sender_of(me, row_index >> 3)
            place_col = jnp.sum(jnp.where(lane == mine_from, place_row, 0.0), axis=1, keepdims=True)
            position = place_col * BLOCK + (row_index & 7).astype(jnp.float32)
            qplace[...] = row - (shard * SHARD).astype(jnp.float32)
            here = (shard * SHARD).astype(jnp.float32) + position
            for g in range(G):
                qhi[g] = here[g * ROWS:(g + 1) * ROWS]

    my_docs = docs[pl.ds(lax.div(me, 2), 1), :].astype(jnp.float32)
    at = iota((N, 1), 0)
    doc_col = jnp.sum(jnp.where(lane == at + shift, my_docs, 0.0), axis=1, keepdims=True)

    def count(r, total):
        return total + jnp.where(docs[pl.ds(r, 1), :].astype(jnp.float32) < doc_col, 1.0, 0.0)

    counted = lax.fori_loop(0, 32, count, jnp.zeros((N, 128), jnp.float32))
    start_col = jnp.sum(counted, axis=1, keepdims=True) * BLOCK
    start_row = jnp.sum(jnp.where(lane == at, start_col, 0.0), axis=0, keepdims=True)
    low = jnp.sum(jnp.where(lane.astype(jnp.float32) == place_col, start_row, 0.0), axis=1, keepdims=True)
    for g in range(G):
        qlo[g] = low[g * ROWS:(g + 1) * ROWS]

    m_ref[...] = jnp.full_like(m_ref, NEG)
    l_ref[...] = jnp.zeros_like(l_ref)
    o_ref[...] = jnp.zeros_like(o_ref)

    def project_part(g, part, peer):
        piece = xg[part, group(g)].astype(jnp.float32)
        lhs = jnp.concatenate(
            [piece[:, :BLOCK].reshape(ROWS, HALF), piece[:, BLOCK:].reshape(ROWS, HALF)], axis=1
        ).astype(jnp.bfloat16)
        depth = pl.ds(pl.multiple_of(peer * DEPTH, DEPTH), DEPTH)
        acc[:, :QW] += jnp.dot(lhs, wq[depth, :], preferred_element_type=jnp.float32)
        acc[:, QW:] += jnp.dot(lhs, wkv[depth, :], preferred_element_type=jnp.float32)

    def project(g):
        acc[...] = jnp.concatenate(
            [jnp.broadcast_to(b[h:h + 1, :], (ROWS, HEAD_SIZE)) for b in (bq, bkv) for h in range(b.shape[0])], axis=1)

        @pl.loop(0, 4)
        def _(part):
            @pl.when(part == 3)
            def _():
                relay(g, 0).wait_recv()
                relay(g, 1).wait_recv()

            shift = jnp.where(part == 3, 2, jnp.where(part == 1, X - 1, jnp.where(part == 2, 1, 0)))
            project_part(g, part, lax.rem(x + shift, X))

        for h in range(HEADS):
            qs[g, pl.ds(h * ROWS, ROWS), :] = acc[:, h * HEAD_SIZE:(h + 1) * HEAD_SIZE].astype(jnp.bfloat16)
        kv[0, g] = acc[:, QW:].astype(jnp.bfloat16)
        kv_copy(g, 0).start()

    def attend(i, j):
        keys = jnp.concatenate(
            [kv[h, j][:, :HEAD_SIZE] for h in range(4)] + [pb[h, j][:, :HEAD_SIZE] for h in range(3)], axis=0)
        values = jnp.concatenate(
            [kv[h, j][:, HEAD_SIZE:] for h in range(4)] + [pb[h, j][:, HEAD_SIZE:] for h in range(3)], axis=0)
        place = kpos[j]
        bias = jnp.where((place <= qhi[i]) & (place >= qlo[i]), 0.0, NEG)
        s = lax.dot_general(qs[i], keys, (((1,), (1,)), ((), ())), preferred_element_type=jnp.float32)
        s = (s.reshape(HEADS, ROWS, KEYS) + bias[None]).reshape(HEADS * ROWS, KEYS)
        m_old = m_ref[i]
        m_new = jnp.maximum(m_old, jnp.max(s, axis=1, keepdims=True))
        p = jnp.exp2((s - m_new[:, :1]) * SCALE)
        alpha = jnp.exp2((m_old - m_new) * SCALE)
        l_ref[i] = l_ref[i] * alpha + jnp.sum(p, axis=1, keepdims=True)
        o_ref[i] = o_ref[i] * alpha + jnp.dot(p.astype(jnp.bfloat16), values, preferred_element_type=jnp.float32)
        m_ref[i] = m_new

    group_ready(0)
    load_wq.wait()

    @pl.loop(0, G + 2)
    def _(step):
        @pl.when(step >= 2)
        def _():
            j = step - 2
            chain_end(j)
            rows_there = jnp.minimum(step, G)
            older = jnp.where(step <= G, j, 0)

            @pl.loop(0, rows_there + older)
            def _(t):
                i = jnp.where(t < rows_there, t, rows_there - 1)
                jj = jnp.where(t < rows_there, j, t - rows_there)
                attend(i, jj)

        @pl.when(step < G)
        def _():
            x_send(step, 0).wait_recv()
            relay(step, 0).start()
            x_send(step, 1).wait_recv()
            relay(step, 1).start()

        @pl.when(step + 1 < G)
        def _():
            group_ready(step + 1)

        @pl.when((step >= 1) & (step <= G))
        def _():
            chain(step - 1, 1)

        @pl.when(step < G)
        def _():
            project(step)

        @pl.when((step >= 1) & (step <= G))
        def _():
            chain(step - 1, 2)
            chain(step - 1, 3)

    @pl.loop(0, G)
    def _(g):
        for h in range(HEADS):
            rows = pl.ds(h * ROWS, ROWS)
            part = o_ref[g, rows, :] / l_ref[g, rows, :]
            on[pl.ds(g * ROWS, ROWS), h * HEAD_SIZE:(h + 1) * HEAD_SIZE] = part.astype(jnp.bfloat16)

    order = jnp.where(iota((SHARD, 1), 0).astype(jnp.float32) == qplace[...], 1.0, 0.0).astype(jnp.bfloat16)
    out[...] = jnp.dot(order, on[...], preferred_element_type=jnp.float32).astype(jnp.bfloat16)

    pltpu.make_async_copy(send.at[pl.ds(1, N - 1)], send.at[pl.ds(1, N - 1)], a2a_send).wait()

    @pl.loop(0, G)
    def _(g):
        for side in range(2):
            x_send(g, side).wait_send()
            relay(g, side).wait_send()
        for h in range(3):
            kv_copy(g, h).wait_send()
            pb_copy(g, h).wait_send()


def per_device(tokens, w_query, key_value_weight, bias_query, key_value_bias, destination, doc_ids):
    vmem, hbm = (pl.BlockSpec(memory_space=s) for s in (pltpu.VMEM, pl.ANY))
    bf16, f32 = jnp.bfloat16, jnp.float32
    dma = pltpu.SemaphoreType.DMA
    return pl.pallas_call(
        kernel,
        out_shape=jax.ShapeDtypeStruct((SHARD, QW), bf16),
        in_specs=[vmem, vmem, vmem, vmem, hbm, hbm, hbm],
        out_specs=vmem,
        scratch_shapes=[
            pltpu.VMEM((SHARD, DEPTH), bf16),
            pltpu.VMEM((N, 2 * BLOCK, HALF), bf16),
            pltpu.VMEM((X, N, 2 * BLOCK, HALF), bf16),
            pltpu.VMEM((X * DEPTH, QW), bf16),
            pltpu.VMEM((2 * X * DEPTH, HEAD_SIZE), bf16),
            pltpu.VMEM((X * DEPTH, 2 * HEAD_SIZE), bf16),
            pltpu.VMEM((ROWS, QW + 2 * HEAD_SIZE), f32),
            pltpu.VMEM((G, HEADS * ROWS, HEAD_SIZE), bf16),
            pltpu.VMEM((4, G, ROWS, 2 * HEAD_SIZE), bf16),
            pltpu.VMEM((3, G, ROWS, 2 * HEAD_SIZE), bf16),
            pltpu.VMEM((G, HEADS * ROWS, HEAD_SIZE), f32),
            pltpu.VMEM((G, HEADS * ROWS, HEAD_SIZE), f32),
            pltpu.VMEM((G, HEADS * ROWS, HEAD_SIZE), f32),
            pltpu.VMEM((SHARD, QW), bf16),
            pltpu.VMEM((512, HEAD_SIZE), f32),
            pltpu.VMEM((G, 1, KEYS), f32),
            pltpu.VMEM((G, ROWS, 1), f32),
            pltpu.VMEM((G, ROWS, 1), f32),
            pltpu.VMEM((1, SHARD), f32),
            dma((3,)), dma, dma((G,)),
            dma((2, G)), dma((2, G)), dma((2, G)), dma((2, G)),
            dma((3, G)), dma((3, G)), dma((3, G)), dma((3, G)),
        ],
        compiler_params=pltpu.CompilerParams(
            collective_id=0, has_side_effects=True, vmem_limit_bytes=56 * 1024 * 1024),
    )(destination.reshape(N // 2, 128), doc_ids.reshape(N // 2, 128), bias_query.reshape(HEADS, HEAD_SIZE), key_value_bias,
      tokens, w_query, key_value_weight.reshape(2 * X * DEPTH, HEAD_SIZE))


def solution(mesh):
    placed = (
        P("ctx", "head"),
        P(None, "head"),
        P(None, None, "head"),
        P("head"),
        P(None, "head"),
        P(),
        P(),
    )
    return jax.shard_map(
        per_device, mesh=mesh, in_specs=placed, out_specs=P("ctx", "head"), check_vma=False
    )
```

```python
import functools
import math

import jax
import jax.numpy as jnp
from jax import lax
from jax.experimental import pallas as pl
from jax.experimental.pallas import tpu as pltpu
from jax.sharding import PartitionSpec as P

MESH = pl.DeviceIdType.MESH
HEAD_SIZE = 128
HEADS = 5
BLOCK = 8
Y, Z, C, X = 4, 8, 2, 4
N = Y * Z * C
G = 4
PER = N // G
ROWS = PER * BLOCK
SHARD = N * BLOCK
HALF = 640
DEPTH = 2 * HALF
QW = HEADS * HEAD_SIZE
DISTANCES = (0, 2, 4, 6, 1, 3, 5)
NBUF = len(DISTANCES)
KEYS = NBUF * ROWS
NEG = -1e30
SCALE = 1.0 / math.sqrt(HEAD_SIZE) * math.log2(math.e)


def slot_parts(slot):
    dz, dc = (slot >> 1) & (Z - 1), slot & 1
    return ((slot >> 4) + dz) & (Y - 1), dz, dc


def sender_of(ctx, slot):
    dy, dz, dc = slot_parts(slot)
    return ((((ctx >> 4) - dy) & (Y - 1)) << 4) + ((((ctx >> 1) - dz) & (Z - 1)) << 1) + ((ctx - dc) & 1)


def target_of(ctx, slot):
    dy, dz, dc = slot_parts(slot)
    return ((((ctx >> 4) + dy) & (Y - 1)) << 4) + ((((ctx >> 1) + dz) & (Z - 1)) << 1) + ((ctx + dc) & 1)


def iota(shape, dim):
    return lax.broadcasted_iota(jnp.int32, shape, dim)


def kernel(table, docs, bq, bkv, tokens, wq_hbm, wkv_hbm, out,
           tok, send, xg, wq, wraw, wkv, acc, qs, kv, pb, m_ref, l_ref, o_ref, stage,
           kpos, qlo, qhi, qplace,
           local_sem, a2a_send, a2a_recv, xs_send, x_recv, rl_send, rl_recv,
           kv_send, kv_recv, pb_send, pb_recv):
    me = lax.axis_index("ctx")
    x = lax.axis_index("head")
    core = lax.rem(me, C)
    my_y, my_z = lax.div(me, Z * C), lax.rem(lax.div(me, C), Z)
    right, left = lax.rem(x + 1, X), lax.rem(x + X - 1, X)
    onward = lax.rem(me + C, N)
    onward2 = lax.rem(me + 2 * C, N)
    partner = me + 1 - 2 * core

    load_tok = pltpu.make_async_copy(tokens, tok, local_sem.at[0])
    load_wq = pltpu.make_async_copy(wq_hbm, wq, local_sem.at[1])
    load_wkv = pltpu.make_async_copy(wkv_hbm, wraw, local_sem.at[2])
    load_tok.start()
    load_wkv.start()
    load_wq.start()

    barrier = pltpu.get_barrier_semaphore()

    def chip_at(u):
        g, dz = lax.div(u, Z), lax.rem(u, Z)
        return (lax.rem(my_y + lax.rem(g + dz, Y), Y) * Z + lax.rem(my_z + dz, Z)) * C

    def cores_at(u):
        chip = chip_at(u)
        return (2 * u, chip + core), (2 * u + 1, chip + 1 - core)

    pl.semaphore_signal(barrier, inc=1, device_id=(partner, x), device_id_type=MESH)

    @pl.loop(1, N // 2)
    def _(u):
        for _, target in cores_at(u):
            pl.semaphore_signal(barrier, inc=1, device_id=(target, x), device_id_type=MESH)

    pl.semaphore_signal(barrier, inc=1, device_id=(me, right), device_id_type=MESH)
    pl.semaphore_signal(barrier, inc=1, device_id=(me, left), device_id_type=MESH)

    shift = (me & 1) * N
    mine = table[pl.ds(lax.div(me, 2), 1), :]
    spread = jnp.where(iota((128, SHARD), 0) == shift + (iota((128, SHARD), 1) >> 3), 1.0, 0.0).astype(jnp.bfloat16)
    owners = jnp.broadcast_to((mine >> 6).astype(jnp.float32).astype(jnp.bfloat16), (8, 128))
    owner_of = jnp.dot(owners, spread, preferred_element_type=jnp.float32)[0:1].astype(jnp.int32)
    load_tok.wait()
    for g in range(G):
        row = iota((ROWS, 1), 0)
        target = target_of(me, (row >> 3) + g * PER)
        pick = (owner_of == target) & ((iota((1, SHARD), 1) & 7) == (row & 7))
        picked = jnp.dot(jnp.where(pick, 1.0, 0.0).astype(jnp.bfloat16), tok[...], preferred_element_type=jnp.float32)
        halves = [picked[:, h * HALF:(h + 1) * HALF].reshape(PER, BLOCK, HALF) for h in range(2)]
        send[pl.ds(g * PER, PER)] = jnp.concatenate(halves, axis=1).astype(jnp.bfloat16)

    pl.semaphore_wait(barrier, N + 1)

    def a2a(s, target):
        return pltpu.make_async_remote_copy(
            src_ref=send.at[s], dst_ref=xg.at[0, s], send_sem=a2a_send, recv_sem=a2a_recv.at[lax.div(s, PER)],
            device_id=(target, x), device_id_type=MESH)

    own = pltpu.make_async_copy(send.at[0], xg.at[0, 0], a2a_recv.at[0])
    own.start()
    a2a(1, partner).start()

    @pl.loop(1, N // 2)
    def _(u):
        for s, target in cores_at(u):
            a2a(s, target).start()

    def group(g):
        return pl.ds(g * PER, PER)

    def x_send(g, side):
        return pltpu.make_async_remote_copy(
            src_ref=xg.at[0, group(g)], dst_ref=xg.at[1 + side, group(g)],
            send_sem=xs_send.at[side, g], recv_sem=x_recv.at[side, g],
            device_id=(me, right if side == 0 else left), device_id_type=MESH)

    def relay(g, side):
        half = pl.ds(g * PER + side * (PER // 2), PER // 2)
        return pltpu.make_async_remote_copy(
            src_ref=xg.at[1 + side, half], dst_ref=xg.at[3, half],
            send_sem=rl_send.at[side, g], recv_sem=rl_recv.at[side, g],
            device_id=(me, right if side == 0 else left), device_id_type=MESH)

    def kv_copy(g, h):
        return pltpu.make_async_remote_copy(
            src_ref=kv.at[min(h, 1), g], dst_ref=kv.at[h + 1, g],
            send_sem=kv_send.at[h, g], recv_sem=kv_recv.at[h, g],
            device_id=(onward2 if h == 2 else onward, x), device_id_type=MESH)

    def pb_copy(g, i):
        return pltpu.make_async_remote_copy(
            src_ref=kv.at[i + core, g], dst_ref=pb.at[i, g],
            send_sem=pb_send.at[i, g], recv_sem=pb_recv.at[i, g],
            device_id=(partner, x), device_id_type=MESH)

    def group_ready(g):
        pltpu.make_async_copy(xg.at[0, group(g)], xg.at[0, group(g)], a2a_recv.at[g]).wait()
        x_send(g, 0).start()
        x_send(g, 1).start()

    def pass_on(g):
        kv_copy(g, 0).wait_recv()
        kv_copy(g, 1).start()
        kv_copy(g, 2).start()
        pb_copy(g, 0).start()

    def share(g):
        for h in (1, 2):
            kv_copy(g, h).wait_recv()
            pb_copy(g, h).start()

    def chain_end(g):
        for i in range(3):
            pb_copy(g, i).wait_recv()

    load_wkv.wait()

    @pl.loop(0, 20)
    def _(t):
        raw = wraw[pl.ds(t * 512, 512), :].astype(jnp.float32)
        stage[...] = raw
        rows = pl.ds(t * 256, 256)
        wkv[rows, :HEAD_SIZE] = stage[pl.ds(0, 256, 2), :].astype(jnp.bfloat16)
        wkv[rows, HEAD_SIZE:] = stage[pl.ds(1, 256, 2), :].astype(jnp.bfloat16)

    entry = table[...]
    entry_place = (entry & (N - 1)).astype(jnp.float32)
    lane = iota((1, 128), 1)
    lane_slot = iota((1, SHARD), 1) >> 3
    lane_token = (iota((1, SHARD), 1) & 7).astype(jnp.float32)
    pair = iota((N // 2, 1), 0)
    eye = iota((ROWS, ROWS), 0) == iota((ROWS, ROWS), 1)
    for buf, distance in enumerate(DISTANCES):
        shard = me - distance
        wrapped = shard & (N - 1)
        found = jnp.where((entry >> 6) == wrapped, entry_place, 0.0)
        even = jnp.sum(jnp.where(lane < N, found, 0.0), axis=1, keepdims=True)
        odd = jnp.sum(jnp.where(lane < N, 0.0, found), axis=1, keepdims=True)
        sender = sender_of(wrapped, lane_slot)
        hit = (sender >> 1) == pair
        place = jnp.sum(jnp.where(hit, jnp.where((sender & 1) == 0, even, odd), 0.0), axis=0, keepdims=True)
        row = (shard * SHARD).astype(jnp.float32) + place * BLOCK + lane_token
        for g in range(G):
            across = jnp.where(eye, row[:, g * ROWS:(g + 1) * ROWS], 0.0)
            kpos[g, buf * ROWS:(buf + 1) * ROWS, :] = jnp.sum(across, axis=1, keepdims=True)
            if buf == 0:
                qhi[g] = row[:, g * ROWS:(g + 1) * ROWS]
        if buf == 0:
            qplace[...] = row - (shard * SHARD).astype(jnp.float32)
            own_place = place

    my_docs = docs[pl.ds(lax.div(me, 2), 1), :].astype(jnp.float32)
    at = iota((N, 1), 0)
    doc_col = jnp.sum(jnp.where(lane == at + shift, my_docs, 0.0), axis=1, keepdims=True)

    def count(r, total):
        return total + jnp.where(docs[pl.ds(r, 1), :].astype(jnp.float32) < doc_col, 1.0, 0.0)

    counted = lax.fori_loop(0, 32, count, jnp.zeros((N, 128), jnp.float32))
    start_col = jnp.sum(counted, axis=1, keepdims=True) * BLOCK
    low = jnp.sum(jnp.where(own_place == at.astype(jnp.float32), start_col, 0.0), axis=0, keepdims=True)
    for g in range(G):
        qlo[g] = low[:, g * ROWS:(g + 1) * ROWS]

    m_ref[...] = jnp.full_like(m_ref, NEG)
    l_ref[...] = jnp.zeros_like(l_ref)
    o_ref[...] = jnp.zeros_like(o_ref)

    def project_part(g, part, peer):
        piece = xg[part, group(g)].astype(jnp.float32)
        lhs = jnp.concatenate(
            [piece[:, :BLOCK].reshape(ROWS, HALF), piece[:, BLOCK:].reshape(ROWS, HALF)], axis=1
        ).astype(jnp.bfloat16)
        depth = pl.ds(pl.multiple_of(peer * DEPTH, DEPTH), DEPTH)
        acc[:, :QW] += jnp.dot(lhs, wq[depth, :], preferred_element_type=jnp.float32)
        acc[:, QW:] += jnp.dot(lhs, wkv[depth, :], preferred_element_type=jnp.float32)

    def project(g):
        acc[...] = jnp.concatenate(
            [jnp.broadcast_to(b[h:h + 1, :], (ROWS, HEAD_SIZE)) for b in (bq, bkv) for h in range(b.shape[0])], axis=1)

        @pl.loop(0, 4)
        def _(part):
            @pl.when(part == 3)
            def _():
                relay(g, 0).wait_recv()
                relay(g, 1).wait_recv()

            shift = jnp.where(part == 3, 2, jnp.where(part == 1, X - 1, jnp.where(part == 2, 1, 0)))
            project_part(g, part, lax.rem(x + shift, X))

        for h in range(HEADS):
            qs[g, pl.ds(h * ROWS, ROWS), :] = acc[:, h * HEAD_SIZE:(h + 1) * HEAD_SIZE].astype(jnp.bfloat16)
        kv[0, g] = jnp.concatenate(
            [acc[:, QW:QW + HEAD_SIZE], acc[:, QW + HEAD_SIZE:].T], axis=1).astype(jnp.bfloat16)
        kv_copy(g, 0).start()

    def attend(i, j):
        blocks = [kv[h, j] for h in range(4)] + [pb[h, j] for h in range(3)]
        keys = jnp.concatenate([block[:, :HEAD_SIZE] for block in blocks], axis=0)
        values = jnp.concatenate([block[:, HEAD_SIZE:] for block in blocks], axis=1)
        values = jnp.concatenate([values, jnp.ones((16, KEYS), jnp.bfloat16)], axis=0)
        place = kpos[j]
        bias = jnp.where((place <= qhi[i]) & (place >= qlo[i]), 0.0, NEG)
        s = lax.dot_general(keys, qs[i], (((1,), (1,)), ((), ())), preferred_element_type=jnp.float32)
        s = s + jnp.concatenate([bias] * HEADS, axis=1)
        m_old = m_ref[i]
        m_new = jnp.maximum(m_old, jnp.max(s, axis=0, keepdims=True))
        p = jnp.exp2((s - m_new) * SCALE).astype(jnp.bfloat16)
        alpha = jnp.exp2((m_old - m_new) * SCALE)
        added = jnp.dot(values, p, preferred_element_type=jnp.float32)
        o_ref[i] = o_ref[i] * alpha + added[:HEAD_SIZE]
        l_ref[i] = l_ref[i] * alpha + added[HEAD_SIZE:HEAD_SIZE + 1]
        m_ref[i] = m_new

    group_ready(0)
    load_wq.wait()
    group_ready(1)

    @pl.loop(0, G + 3)
    def _(step):
        @pl.when(step < G)
        def _():
            for side in range(2):
                x_send(step, side).wait_recv()
                relay(step, side).start()

        @pl.when(step + 2 < G)
        def _():
            group_ready(step + 2)

        @pl.when((step >= 2) & (step <= G))
        def _():
            pass_on(step - 2)

        @pl.when((step >= 1) & (step <= G))
        def _():
            project(step - 1)

        @pl.when(step >= 3)
        def _():
            chain_end(step - 3)

        j = step - 3
        there = jnp.minimum(step, G)
        pairs = jnp.where(step < 3, 0, there + jnp.where(step <= G, j, 0))

        @pl.loop(0, 3)
        def _(third):
            @pl.when((third == 2) & (step == G))
            def _():
                pass_on(step - 1)

            @pl.when((third == 2) & (step == G + 1))
            def _():
                share(step - 2)

            @pl.loop(lax.div(pairs * third, 3), lax.div(pairs * (third + 1), 3))
            def _(t):
                attend(jnp.where(t < there, t, there - 1), jnp.where(t < there, j, t - there))

        @pl.when((step >= 2) & (step <= G))
        def _():
            share(step - 2)

    order = jnp.where(iota((SHARD, 1), 0).astype(jnp.float32) == qplace[...], 1.0, 0.0).astype(jnp.bfloat16)
    for h in range(HEADS):
        columns = slice(h * HEAD_SIZE, (h + 1) * HEAD_SIZE)
        part = jnp.concatenate([o_ref[g, :, columns] / l_ref[g, :, columns] for g in range(G)], axis=1)
        out[:, columns] = lax.dot_general(
            order, part.astype(jnp.bfloat16), (((1,), (1,)), ((), ())), preferred_element_type=jnp.float32
        ).astype(jnp.bfloat16)

    pltpu.make_async_copy(send.at[pl.ds(1, N - 1)], send.at[pl.ds(1, N - 1)], a2a_send).wait()

    @pl.loop(0, G)
    def _(g):
        for side in range(2):
            x_send(g, side).wait_send()
            relay(g, side).wait_send()
        for h in range(3):
            kv_copy(g, h).wait_send()
            pb_copy(g, h).wait_send()


def per_device(tokens, w_query, key_value_weight, bias_query, key_value_bias, destination, doc_ids):
    vmem, hbm = (pl.BlockSpec(memory_space=s) for s in (pltpu.VMEM, pl.ANY))
    bf16, f32 = jnp.bfloat16, jnp.float32
    dma = pltpu.SemaphoreType.DMA
    return pl.pallas_call(
        kernel,
        out_shape=jax.ShapeDtypeStruct((SHARD, QW), bf16),
        in_specs=[vmem, vmem, vmem, vmem, hbm, hbm, hbm],
        out_specs=vmem,
        scratch_shapes=[
            pltpu.VMEM((SHARD, DEPTH), bf16),
            pltpu.VMEM((N, 2 * BLOCK, HALF), bf16),
            pltpu.VMEM((X, N, 2 * BLOCK, HALF), bf16),
            pltpu.VMEM((X * DEPTH, QW), bf16),
            pltpu.VMEM((2 * X * DEPTH, HEAD_SIZE), bf16),
            pltpu.VMEM((X * DEPTH, 2 * HEAD_SIZE), bf16),
            pltpu.VMEM((ROWS, QW + 2 * HEAD_SIZE), f32),
            pltpu.VMEM((G, HEADS * ROWS, HEAD_SIZE), bf16),
            pltpu.VMEM((4, G, ROWS, 2 * HEAD_SIZE), bf16),
            pltpu.VMEM((3, G, ROWS, 2 * HEAD_SIZE), bf16),
            pltpu.VMEM((G, 1, HEADS * ROWS), f32),
            pltpu.VMEM((G, 1, HEADS * ROWS), f32),
            pltpu.VMEM((G, HEAD_SIZE, HEADS * ROWS), f32),
            pltpu.VMEM((512, HEAD_SIZE), f32),
            pltpu.VMEM((G, KEYS, 1), f32),
            pltpu.VMEM((G, 1, ROWS), f32),
            pltpu.VMEM((G, 1, ROWS), f32),
            pltpu.VMEM((1, SHARD), f32),
            dma((3,)), dma, dma((G,)),
            dma((2, G)), dma((2, G)), dma((2, G)), dma((2, G)),
            dma((3, G)), dma((3, G)), dma((3, G)), dma((3, G)),
        ],
        compiler_params=pltpu.CompilerParams(
            collective_id=0, has_side_effects=True, vmem_limit_bytes=56 * 1024 * 1024),
    )(destination.reshape(N // 2, 128), doc_ids.reshape(N // 2, 128), bias_query.reshape(HEADS, HEAD_SIZE), key_value_bias,
      tokens, w_query, key_value_weight.reshape(2 * X * DEPTH, HEAD_SIZE))


def solution(mesh):
    placed = (
        P("ctx", "head"),
        P(None, "head"),
        P(None, None, "head"),
        P("head"),
        P(None, "head"),
        P(),
        P(),
    )
    return jax.shard_map(
        per_device, mesh=mesh, in_specs=placed, out_specs=P("ctx", "head"), check_vma=False
    )
```

```python
import functools
import math

import jax
import jax.numpy as jnp
from jax import lax
from jax.experimental import pallas as pl
from jax.experimental.pallas import tpu as pltpu
from jax.sharding import PartitionSpec as P

MESH = pl.DeviceIdType.MESH
HEAD_SIZE = 128
HEADS = 5
BLOCK = 8
Y, Z, C, X = 4, 8, 2, 4
N = Y * Z * C
G = 4
PER = N // G
ROWS = PER * BLOCK
SHARD = N * BLOCK
HALF = 640
DEPTH = 2 * HALF
QW = HEADS * HEAD_SIZE
DISTANCES = (0, 2, 4, 6, 1, 3, 5)
NBUF = len(DISTANCES)
KEYS = NBUF * ROWS
NEG = -1e30
SCALE = 1.0 / math.sqrt(HEAD_SIZE) * math.log2(math.e)


def slot_parts(slot):
    order = slot >> 3
    dz = (((order + 1) >> 1) * (2 * (order & 1) - 1)) & (Z - 1)
    return (slot >> 1) & (Y - 1), dz, slot & 1


def sender_of(ctx, slot):
    dy, dz, dc = slot_parts(slot)
    return ((((ctx >> 4) - dy) & (Y - 1)) << 4) + ((((ctx >> 1) - dz) & (Z - 1)) << 1) + ((ctx - dc) & 1)


def target_of(ctx, slot):
    dy, dz, dc = slot_parts(slot)
    return ((((ctx >> 4) + dy) & (Y - 1)) << 4) + ((((ctx >> 1) + dz) & (Z - 1)) << 1) + ((ctx + dc) & 1)


def iota(shape, dim):
    return lax.broadcasted_iota(jnp.int32, shape, dim)


def kernel(table, docs, bq, bkv, tokens, wq_hbm, wkv_hbm, out,
           tok, send, xg, wq, wraw, wkv, acc, qs, kv, pb, m_ref, l_ref, o_ref, stage,
           kpos, qlo, qhi, qplace,
           local_sem, a2a_send, a2a_recv, xs_send, x_recv, rl_send, rl_recv,
           kv_send, kv_recv, pb_send, pb_recv):
    me = lax.axis_index("ctx")
    x = lax.axis_index("head")
    core = lax.rem(me, C)
    my_y, my_z = lax.div(me, Z * C), lax.rem(lax.div(me, C), Z)
    right, left = lax.rem(x + 1, X), lax.rem(x + X - 1, X)
    onward = lax.rem(me + C, N)
    onward2 = lax.rem(me + 2 * C, N)
    partner = me + 1 - 2 * core

    load_tok = pltpu.make_async_copy(tokens, tok, local_sem.at[0])
    load_wq = pltpu.make_async_copy(wq_hbm, wq, local_sem.at[1])
    load_wkv = pltpu.make_async_copy(wkv_hbm, wraw, local_sem.at[2])
    load_tok.start()
    load_wkv.start()
    load_wq.start()

    barrier = pltpu.get_barrier_semaphore()

    def chip_at(u):
        order, dy = lax.div(u, Y), lax.rem(u, Y)
        dz = Z + lax.div(order + 1, 2) * (2 * lax.rem(order, 2) - 1)
        return (lax.rem(my_y + dy, Y) * Z + lax.rem(my_z + dz, Z)) * C

    def cores_at(u):
        chip = chip_at(u)
        return (2 * u, chip + core), (2 * u + 1, chip + 1 - core)

    pl.semaphore_signal(barrier, inc=1, device_id=(partner, x), device_id_type=MESH)

    @pl.loop(1, N // 2)
    def _(u):
        for _, target in cores_at(u):
            pl.semaphore_signal(barrier, inc=1, device_id=(target, x), device_id_type=MESH)

    pl.semaphore_signal(barrier, inc=1, device_id=(me, right), device_id_type=MESH)
    pl.semaphore_signal(barrier, inc=1, device_id=(me, left), device_id_type=MESH)

    shift = (me & 1) * N
    mine = table[pl.ds(lax.div(me, 2), 1), :]
    spread = jnp.where(iota((128, SHARD), 0) == shift + (iota((128, SHARD), 1) >> 3), 1.0, 0.0).astype(jnp.bfloat16)
    owners = jnp.broadcast_to((mine >> 6).astype(jnp.float32).astype(jnp.bfloat16), (8, 128))
    owner_of = jnp.dot(owners, spread, preferred_element_type=jnp.float32)[0:1].astype(jnp.int32)
    load_tok.wait()

    def a2a(s, target):
        return pltpu.make_async_remote_copy(
            src_ref=send.at[s], dst_ref=xg.at[0, s], send_sem=a2a_send, recv_sem=a2a_recv.at[lax.div(s, PER)],
            device_id=(target, x), device_id_type=MESH)

    for g in range(G):
        row = iota((ROWS, 1), 0)
        target = target_of(me, (row >> 3) + g * PER)
        pick = (owner_of == target) & ((iota((1, SHARD), 1) & 7) == (row & 7))
        picked = jnp.dot(jnp.where(pick, 1.0, 0.0).astype(jnp.bfloat16), tok[...], preferred_element_type=jnp.float32)
        halves = [picked[:, h * HALF:(h + 1) * HALF].reshape(PER, BLOCK, HALF) for h in range(2)]
        send[pl.ds(g * PER, PER)] = jnp.concatenate(halves, axis=1).astype(jnp.bfloat16)
        if g == 0:
            pl.semaphore_wait(barrier, N + 1)
            pltpu.make_async_copy(send.at[0], xg.at[0, 0], a2a_recv.at[0]).start()
            a2a(1, partner).start()

        @pl.loop(max(1, g * PER // 2), (g + 1) * PER // 2)
        def _(u):
            for s, to in cores_at(u):
                a2a(s, to).start()

    def group(g):
        return pl.ds(g * PER, PER)

    def x_send(g, side):
        return pltpu.make_async_remote_copy(
            src_ref=xg.at[0, group(g)], dst_ref=xg.at[1 + side, group(g)],
            send_sem=xs_send.at[side, g], recv_sem=x_recv.at[side, g],
            device_id=(me, right if side == 0 else left), device_id_type=MESH)

    def relay(g, side):
        half = pl.ds(g * PER + side * (PER // 2), PER // 2)
        return pltpu.make_async_remote_copy(
            src_ref=xg.at[1 + side, half], dst_ref=xg.at[3, half],
            send_sem=rl_send.at[side, g], recv_sem=rl_recv.at[side, g],
            device_id=(me, right if side == 0 else left), device_id_type=MESH)

    def kv_copy(g, h):
        return pltpu.make_async_remote_copy(
            src_ref=kv.at[min(h, 1), g], dst_ref=kv.at[h + 1, g],
            send_sem=kv_send.at[h, g], recv_sem=kv_recv.at[h, g],
            device_id=(onward2 if h == 2 else onward, x), device_id_type=MESH)

    def pb_copy(g, i):
        return pltpu.make_async_remote_copy(
            src_ref=kv.at[i + core, g], dst_ref=pb.at[i, g],
            send_sem=pb_send.at[i, g], recv_sem=pb_recv.at[i, g],
            device_id=(partner, x), device_id_type=MESH)

    def group_ready(g):
        pltpu.make_async_copy(xg.at[0, group(g)], xg.at[0, group(g)], a2a_recv.at[g]).wait()
        x_send(g, 0).start()
        x_send(g, 1).start()

    def pass_on(g):
        kv_copy(g, 0).wait_recv()
        kv_copy(g, 1).start()
        kv_copy(g, 2).start()
        pb_copy(g, 0).start()

    def share(g):
        for h in (1, 2):
            kv_copy(g, h).wait_recv()
            pb_copy(g, h).start()

    def chain_end(g):
        for i in range(3):
            pb_copy(g, i).wait_recv()

    m_ref[...] = jnp.full_like(m_ref, NEG)
    l_ref[...] = jnp.zeros_like(l_ref)
    o_ref[...] = jnp.zeros_like(o_ref)

    def project_part(g, part, peer):
        piece = xg[part, group(g)].astype(jnp.float32)
        lhs = jnp.concatenate(
            [piece[:, :BLOCK].reshape(ROWS, HALF), piece[:, BLOCK:].reshape(ROWS, HALF)], axis=1
        ).astype(jnp.bfloat16)
        depth = pl.ds(pl.multiple_of(peer * DEPTH, DEPTH), DEPTH)
        acc[:, :QW] += jnp.dot(lhs, wq[depth, :], preferred_element_type=jnp.float32)
        acc[:, QW:] += jnp.dot(lhs, wkv[depth, :], preferred_element_type=jnp.float32)

    def project(g):
        acc[...] = jnp.concatenate(
            [jnp.broadcast_to(b[h:h + 1, :], (ROWS, HEAD_SIZE)) for b in (bq, bkv) for h in range(b.shape[0])], axis=1)

        @pl.loop(0, 4)
        def _(part):
            @pl.when(part == 3)
            def _():
                relay(g, 0).wait_recv()
                relay(g, 1).wait_recv()

            shift = jnp.where(part == 3, 2, jnp.where(part == 1, X - 1, jnp.where(part == 2, 1, 0)))
            project_part(g, part, lax.rem(x + shift, X))

        for h in range(HEADS):
            qs[g, pl.ds(h * ROWS, ROWS), :] = acc[:, h * HEAD_SIZE:(h + 1) * HEAD_SIZE].astype(jnp.bfloat16)
        kv[0, g] = jnp.concatenate(
            [acc[:, QW:QW + HEAD_SIZE], acc[:, QW + HEAD_SIZE:].T], axis=1).astype(jnp.bfloat16)
        kv_copy(g, 0).start()

    def attend(i, j):
        blocks = [kv[h, j] for h in range(4)] + [pb[h, j] for h in range(3)]
        keys = jnp.concatenate([block[:, :HEAD_SIZE] for block in blocks], axis=0)
        values = jnp.concatenate([block[:, HEAD_SIZE:] for block in blocks], axis=1)
        values = jnp.concatenate([values, jnp.ones((16, KEYS), jnp.bfloat16)], axis=0)
        place = kpos[j]
        bias = jnp.where((place <= qhi[i]) & (place >= qlo[i]), 0.0, NEG)
        s = lax.dot_general(keys, qs[i], (((1,), (1,)), ((), ())), preferred_element_type=jnp.float32)
        s = s + jnp.concatenate([bias] * HEADS, axis=1)
        m_old = m_ref[i]
        m_new = jnp.maximum(m_old, jnp.max(s, axis=0, keepdims=True))
        p = jnp.exp2((s - m_new) * SCALE).astype(jnp.bfloat16)
        alpha = jnp.exp2((m_old - m_new) * SCALE)
        added = jnp.dot(values, p, preferred_element_type=jnp.float32)
        o_ref[i] = o_ref[i] * alpha + added[:HEAD_SIZE]
        l_ref[i] = l_ref[i] * alpha + added[HEAD_SIZE:HEAD_SIZE + 1]
        m_ref[i] = m_new

    group_ready(0)

    load_wkv.wait()

    @pl.loop(0, 20)
    def _(t):
        raw = wraw[pl.ds(t * 512, 512), :].astype(jnp.float32)
        stage[...] = raw
        rows = pl.ds(t * 256, 256)
        wkv[rows, :HEAD_SIZE] = stage[pl.ds(0, 256, 2), :].astype(jnp.bfloat16)
        wkv[rows, HEAD_SIZE:] = stage[pl.ds(1, 256, 2), :].astype(jnp.bfloat16)

    entry = table[...]
    entry_place = (entry & (N - 1)).astype(jnp.float32)
    lane = iota((1, 128), 1)
    lane_slot = iota((1, SHARD), 1) >> 3
    lane_token = (iota((1, SHARD), 1) & 7).astype(jnp.float32)
    pair = iota((N // 2, 1), 0)
    eye = iota((ROWS, ROWS), 0) == iota((ROWS, ROWS), 1)
    for buf, distance in enumerate(DISTANCES):
        shard = me - distance
        wrapped = shard & (N - 1)
        found = jnp.where((entry >> 6) == wrapped, entry_place, 0.0)
        even = jnp.sum(jnp.where(lane < N, found, 0.0), axis=1, keepdims=True)
        odd = jnp.sum(jnp.where(lane < N, 0.0, found), axis=1, keepdims=True)
        sender = sender_of(wrapped, lane_slot)
        hit = (sender >> 1) == pair
        place = jnp.sum(jnp.where(hit, jnp.where((sender & 1) == 0, even, odd), 0.0), axis=0, keepdims=True)
        row = (shard * SHARD).astype(jnp.float32) + place * BLOCK + lane_token
        for g in range(G):
            across = jnp.where(eye, row[:, g * ROWS:(g + 1) * ROWS], 0.0)
            kpos[g, buf * ROWS:(buf + 1) * ROWS, :] = jnp.sum(across, axis=1, keepdims=True)
            if buf == 0:
                qhi[g] = row[:, g * ROWS:(g + 1) * ROWS]
        if buf == 0:
            qplace[...] = row - (shard * SHARD).astype(jnp.float32)
            own_place = place

    my_docs = docs[pl.ds(lax.div(me, 2), 1), :].astype(jnp.float32)
    at = iota((N, 1), 0)
    doc_col = jnp.sum(jnp.where(lane == at + shift, my_docs, 0.0), axis=1, keepdims=True)

    def count(r, total):
        return total + jnp.where(docs[pl.ds(r, 1), :].astype(jnp.float32) < doc_col, 1.0, 0.0)

    counted = lax.fori_loop(0, 32, count, jnp.zeros((N, 128), jnp.float32))
    start_col = jnp.sum(counted, axis=1, keepdims=True) * BLOCK
    low = jnp.sum(jnp.where(own_place == at.astype(jnp.float32), start_col, 0.0), axis=0, keepdims=True)
    for g in range(G):
        qlo[g] = low[:, g * ROWS:(g + 1) * ROWS]

    group_ready(1)
    load_wq.wait()

    @pl.loop(0, G + 3)
    def _(step):
        @pl.when(step < G)
        def _():
            for side in range(2):
                x_send(step, side).wait_recv()
                relay(step, side).start()

        @pl.when(step + 2 < G)
        def _():
            group_ready(step + 2)

        @pl.when((step >= 2) & (step <= G))
        def _():
            pass_on(step - 2)

        @pl.when((step >= 1) & (step <= G))
        def _():
            project(step - 1)

        @pl.when(step >= 3)
        def _():
            chain_end(step - 3)

        j = step - 3
        there = jnp.minimum(step, G)
        pairs = jnp.where(step < 3, 0, there + jnp.where(step <= G, j, 0))

        @pl.loop(0, 3)
        def _(third):
            @pl.when((third == 2) & (step == G))
            def _():
                pass_on(step - 1)

            @pl.when((third == 2) & (step == G + 1))
            def _():
                share(step - 2)

            @pl.loop(lax.div(pairs * third, 3), lax.div(pairs * (third + 1), 3))
            def _(t):
                attend(jnp.where(t < there, t, there - 1), jnp.where(t < there, j, t - there))

        @pl.when((step >= 2) & (step <= G))
        def _():
            share(step - 2)

    order = jnp.where(iota((SHARD, 1), 0).astype(jnp.float32) == qplace[...], 1.0, 0.0).astype(jnp.bfloat16)
    for h in range(HEADS):
        columns = slice(h * HEAD_SIZE, (h + 1) * HEAD_SIZE)
        part = jnp.concatenate([o_ref[g, :, columns] / l_ref[g, :, columns] for g in range(G)], axis=1)
        out[:, columns] = lax.dot_general(
            order, part.astype(jnp.bfloat16), (((1,), (1,)), ((), ())), preferred_element_type=jnp.float32
        ).astype(jnp.bfloat16)

    pltpu.make_async_copy(send.at[pl.ds(1, N - 1)], send.at[pl.ds(1, N - 1)], a2a_send).wait()

    @pl.loop(0, G)
    def _(g):
        for side in range(2):
            x_send(g, side).wait_send()
            relay(g, side).wait_send()
        for h in range(3):
            kv_copy(g, h).wait_send()
            pb_copy(g, h).wait_send()


def per_device(tokens, w_query, key_value_weight, bias_query, key_value_bias, destination, doc_ids):
    vmem, hbm = (pl.BlockSpec(memory_space=s) for s in (pltpu.VMEM, pl.ANY))
    bf16, f32 = jnp.bfloat16, jnp.float32
    dma = pltpu.SemaphoreType.DMA
    return pl.pallas_call(
        kernel,
        out_shape=jax.ShapeDtypeStruct((SHARD, QW), bf16),
        in_specs=[vmem, vmem, vmem, vmem, hbm, hbm, hbm],
        out_specs=vmem,
        scratch_shapes=[
            pltpu.VMEM((SHARD, DEPTH), bf16),
            pltpu.VMEM((N, 2 * BLOCK, HALF), bf16),
            pltpu.VMEM((X, N, 2 * BLOCK, HALF), bf16),
            pltpu.VMEM((X * DEPTH, QW), bf16),
            pltpu.VMEM((2 * X * DEPTH, HEAD_SIZE), bf16),
            pltpu.VMEM((X * DEPTH, 2 * HEAD_SIZE), bf16),
            pltpu.VMEM((ROWS, QW + 2 * HEAD_SIZE), f32),
            pltpu.VMEM((G, HEADS * ROWS, HEAD_SIZE), bf16),
            pltpu.VMEM((4, G, ROWS, 2 * HEAD_SIZE), bf16),
            pltpu.VMEM((3, G, ROWS, 2 * HEAD_SIZE), bf16),
            pltpu.VMEM((G, 1, HEADS * ROWS), f32),
            pltpu.VMEM((G, 1, HEADS * ROWS), f32),
            pltpu.VMEM((G, HEAD_SIZE, HEADS * ROWS), f32),
            pltpu.VMEM((512, HEAD_SIZE), f32),
            pltpu.VMEM((G, KEYS, 1), f32),
            pltpu.VMEM((G, 1, ROWS), f32),
            pltpu.VMEM((G, 1, ROWS), f32),
            pltpu.VMEM((1, SHARD), f32),
            dma((3,)), dma, dma((G,)),
            dma((2, G)), dma((2, G)), dma((2, G)), dma((2, G)),
            dma((3, G)), dma((3, G)), dma((3, G)), dma((3, G)),
        ],
        compiler_params=pltpu.CompilerParams(
            collective_id=0, has_side_effects=True, vmem_limit_bytes=56 * 1024 * 1024),
    )(destination.reshape(N // 2, 128), doc_ids.reshape(N // 2, 128), bias_query.reshape(HEADS, HEAD_SIZE), key_value_bias,
      tokens, w_query, key_value_weight.reshape(2 * X * DEPTH, HEAD_SIZE))


def solution(mesh):
    placed = (
        P("ctx", "head"),
        P(None, "head"),
        P(None, None, "head"),
        P("head"),
        P(None, "head"),
        P(),
        P(),
    )
    return jax.shard_map(
        per_device, mesh=mesh, in_specs=placed, out_specs=P("ctx", "head"), check_vma=False
    )
```

```python
import functools
import math

import jax
import jax.numpy as jnp
from jax import lax
from jax.experimental import pallas as pl
from jax.experimental.pallas import tpu as pltpu
from jax.sharding import PartitionSpec as P

MESH = pl.DeviceIdType.MESH
HEAD_SIZE = 128
HEADS = 5
BLOCK = 8
Y, Z, C, X = 4, 8, 2, 4
N = Y * Z * C
G = 4
PER = N // G
ROWS = PER * BLOCK
SHARD = N * BLOCK
HALF = 640
DEPTH = 2 * HALF
QW = HEADS * HEAD_SIZE
DISTANCES = (0, 2, 4, 6, 1, 3, 5)
NBUF = len(DISTANCES)
KEYS = NBUF * ROWS
NEG = -1e30
SCALE = 1.0 / math.sqrt(HEAD_SIZE) * math.log2(math.e)


def slot_parts(slot):
    order = slot >> 3
    dz = (((order + 1) >> 1) * (2 * (order & 1) - 1)) & (Z - 1)
    return (slot >> 1) & (Y - 1), dz, slot & 1


def sender_of(ctx, slot):
    dy, dz, dc = slot_parts(slot)
    return ((((ctx >> 4) - dy) & (Y - 1)) << 4) + ((((ctx >> 1) - dz) & (Z - 1)) << 1) + ((ctx - dc) & 1)


def target_of(ctx, slot):
    dy, dz, dc = slot_parts(slot)
    return ((((ctx >> 4) + dy) & (Y - 1)) << 4) + ((((ctx >> 1) + dz) & (Z - 1)) << 1) + ((ctx + dc) & 1)


def iota(shape, dim):
    return lax.broadcasted_iota(jnp.int32, shape, dim)


def kernel(table, docs, bq, bkv, tokens, wq_hbm, wkv_hbm, out,
           tok, send, xg, wq, wraw, wkv, acc, qs, kv, pb, m_ref, l_ref, o_ref, stage,
           kpos, qlo, qhi, qplace,
           local_sem, a2a_send, a2a_recv, xs_send, x_recv, rl_send, rl_recv,
           kv_send, kv_recv, pb_send, pb_recv):
    me = lax.axis_index("ctx")
    x = lax.axis_index("head")
    core = lax.rem(me, C)
    my_y, my_z = lax.div(me, Z * C), lax.rem(lax.div(me, C), Z)
    right, left = lax.rem(x + 1, X), lax.rem(x + X - 1, X)
    onward = lax.rem(me + C, N)
    onward2 = lax.rem(me + 2 * C, N)
    partner = me + 1 - 2 * core

    load_tok = pltpu.make_async_copy(tokens, tok, local_sem.at[0])
    load_wq = pltpu.make_async_copy(wq_hbm, wq, local_sem.at[1])
    load_wkv = pltpu.make_async_copy(wkv_hbm, wraw, local_sem.at[2])
    load_tok.start()
    load_wkv.start()
    load_wq.start()

    barrier = pltpu.get_barrier_semaphore()

    def chip_at(u):
        order, dy = lax.div(u, Y), lax.rem(u, Y)
        dz = Z + lax.div(order + 1, 2) * (2 * lax.rem(order, 2) - 1)
        return (lax.rem(my_y + dy, Y) * Z + lax.rem(my_z + dz, Z)) * C

    def cores_at(u):
        chip = chip_at(u)
        return (2 * u, chip + core), (2 * u + 1, chip + 1 - core)

    pl.semaphore_signal(barrier, inc=1, device_id=(partner, x), device_id_type=MESH)

    @pl.loop(1, N // 2)
    def _(u):
        for _, target in cores_at(u):
            pl.semaphore_signal(barrier, inc=1, device_id=(target, x), device_id_type=MESH)

    pl.semaphore_signal(barrier, inc=1, device_id=(me, right), device_id_type=MESH)
    pl.semaphore_signal(barrier, inc=1, device_id=(me, left), device_id_type=MESH)

    shift = (me & 1) * N
    mine = table[pl.ds(lax.div(me, 2), 1), :]
    spread = jnp.where(iota((128, SHARD), 0) == shift + (iota((128, SHARD), 1) >> 3), 1.0, 0.0).astype(jnp.bfloat16)
    owners = jnp.broadcast_to((mine >> 6).astype(jnp.float32).astype(jnp.bfloat16), (8, 128))
    owner_of = jnp.dot(owners, spread, preferred_element_type=jnp.float32)[0:1].astype(jnp.int32)
    load_tok.wait()

    def a2a(s, target):
        return pltpu.make_async_remote_copy(
            src_ref=send.at[s], dst_ref=xg.at[0, s], send_sem=a2a_send, recv_sem=a2a_recv.at[lax.div(s, PER)],
            device_id=(target, x), device_id_type=MESH)

    for g in range(G):
        row = iota((ROWS, 1), 0)
        target = target_of(me, (row >> 3) + g * PER)
        pick = (owner_of == target) & ((iota((1, SHARD), 1) & 7) == (row & 7))
        picked = jnp.dot(jnp.where(pick, 1.0, 0.0).astype(jnp.bfloat16), tok[...], preferred_element_type=jnp.float32)
        halves = [picked[:, h * HALF:(h + 1) * HALF].reshape(PER, BLOCK, HALF) for h in range(2)]
        send[pl.ds(g * PER, PER)] = jnp.concatenate(halves, axis=1).astype(jnp.bfloat16)
        if g == 0:
            pl.semaphore_wait(barrier, N + 1)
            pltpu.make_async_copy(send.at[0], xg.at[0, 0], a2a_recv.at[0]).start()
            a2a(1, partner).start()

        @pl.loop(max(1, g * PER // 2), (g + 1) * PER // 2)
        def _(u):
            for s, to in cores_at(u):
                a2a(s, to).start()

    def group(g):
        return pl.ds(g * PER, PER)

    def x_send(g, side):
        return pltpu.make_async_remote_copy(
            src_ref=xg.at[0, group(g)], dst_ref=xg.at[1 + side, group(g)],
            send_sem=xs_send.at[side, g], recv_sem=x_recv.at[side, g],
            device_id=(me, right if side == 0 else left), device_id_type=MESH)

    def relay(g, side):
        half = pl.ds(g * PER + side * (PER // 2), PER // 2)
        return pltpu.make_async_remote_copy(
            src_ref=xg.at[1 + side, half], dst_ref=xg.at[3, half],
            send_sem=rl_send.at[side, g], recv_sem=rl_recv.at[side, g],
            device_id=(me, right if side == 0 else left), device_id_type=MESH)

    def kv_copy(g, h):
        return pltpu.make_async_remote_copy(
            src_ref=kv.at[min(h, 1), g], dst_ref=kv.at[h + 1, g],
            send_sem=kv_send.at[h, g], recv_sem=kv_recv.at[h, g],
            device_id=(onward2 if h == 2 else onward, x), device_id_type=MESH)

    def pb_copy(g, i):
        return pltpu.make_async_remote_copy(
            src_ref=kv.at[i + core, g], dst_ref=pb.at[i, g],
            send_sem=pb_send.at[i, g], recv_sem=pb_recv.at[i, g],
            device_id=(partner, x), device_id_type=MESH)

    def group_ready(g):
        pltpu.make_async_copy(xg.at[0, group(g)], xg.at[0, group(g)], a2a_recv.at[g]).wait()
        x_send(g, 0).start()
        x_send(g, 1).start()

    def pass_on(g):
        kv_copy(g, 0).wait_recv()
        kv_copy(g, 1).start()
        kv_copy(g, 2).start()
        pb_copy(g, 0).start()

    def share(g):
        for h in (1, 2):
            kv_copy(g, h).wait_recv()
            pb_copy(g, h).start()

    def chain_end(g):
        for i in range(3):
            pb_copy(g, i).wait_recv()

    m_ref[...] = jnp.full_like(m_ref, NEG)
    l_ref[...] = jnp.zeros_like(l_ref)
    o_ref[...] = jnp.zeros_like(o_ref)

    def project_part(g, part, peer):
        piece = xg[part, group(g)].astype(jnp.float32)
        lhs = jnp.concatenate(
            [piece[:, :BLOCK].reshape(ROWS, HALF), piece[:, BLOCK:].reshape(ROWS, HALF)], axis=1
        ).astype(jnp.bfloat16)
        depth = pl.ds(pl.multiple_of(peer * DEPTH, DEPTH), DEPTH)
        acc[:, :QW] += jnp.dot(lhs, wq[depth, :], preferred_element_type=jnp.float32)
        acc[:, QW:] += jnp.dot(lhs, wkv[depth, :], preferred_element_type=jnp.float32)

    def project(g):
        acc[...] = jnp.concatenate(
            [jnp.broadcast_to(b[h:h + 1, :], (ROWS, HEAD_SIZE)) for b in (bq, bkv) for h in range(b.shape[0])], axis=1)

        @pl.loop(0, 4)
        def _(part):
            @pl.when(part == 3)
            def _():
                relay(g, 0).wait_recv()
                relay(g, 1).wait_recv()

            shift = jnp.where(part == 3, 2, jnp.where(part == 1, X - 1, jnp.where(part == 2, 1, 0)))
            project_part(g, part, lax.rem(x + shift, X))

        for h in range(HEADS):
            qs[g, pl.ds(h * ROWS, ROWS), :] = acc[:, h * HEAD_SIZE:(h + 1) * HEAD_SIZE].astype(jnp.bfloat16)
        kv[0, g] = jnp.concatenate(
            [acc[:, QW:QW + HEAD_SIZE], acc[:, QW + HEAD_SIZE:].T], axis=1).astype(jnp.bfloat16)
        kv_copy(g, 0).start()

    def attend(i, j):
        blocks = [kv[h, j] for h in range(4)] + [pb[h, j] for h in range(3)]
        keys = jnp.concatenate([block[:, :HEAD_SIZE] for block in blocks], axis=0)
        values = jnp.concatenate([block[:, HEAD_SIZE:] for block in blocks], axis=1)
        values = jnp.concatenate([values, jnp.ones((16, KEYS), jnp.bfloat16)], axis=0)
        place = kpos[j]
        bias = jnp.where((place <= qhi[i]) & (place >= qlo[i]), 0.0, NEG)
        s = lax.dot_general(keys, qs[i], (((1,), (1,)), ((), ())), preferred_element_type=jnp.float32)
        s = s + jnp.concatenate([bias] * HEADS, axis=1)
        m_old = m_ref[i]
        m_new = jnp.maximum(m_old, jnp.max(s, axis=0, keepdims=True))
        p = jnp.exp2((s - m_new) * SCALE).astype(jnp.bfloat16)
        alpha = jnp.exp2((m_old - m_new) * SCALE)
        added = jnp.dot(values, p, preferred_element_type=jnp.float32)
        o_ref[i] = o_ref[i] * alpha + added[:HEAD_SIZE]
        l_ref[i] = l_ref[i] * alpha + added[HEAD_SIZE:HEAD_SIZE + 1]
        m_ref[i] = m_new

    group_ready(0)

    load_wkv.wait()

    @pl.loop(0, 20)
    def _(t):
        raw = wraw[pl.ds(t * 512, 512), :].astype(jnp.float32)
        stage[...] = raw
        rows = pl.ds(t * 256, 256)
        wkv[rows, :HEAD_SIZE] = stage[pl.ds(0, 256, 2), :].astype(jnp.bfloat16)
        wkv[rows, HEAD_SIZE:] = stage[pl.ds(1, 256, 2), :].astype(jnp.bfloat16)

    entry = table[...]
    entry_place = (entry & (N - 1)).astype(jnp.float32)
    lane = iota((1, 128), 1)
    lane_slot = iota((1, SHARD), 1) >> 3
    lane_token = (iota((1, SHARD), 1) & 7).astype(jnp.float32)
    pair = iota((N // 2, 1), 0)
    eye = iota((ROWS, ROWS), 0) == iota((ROWS, ROWS), 1)
    for buf, distance in enumerate(DISTANCES):
        shard = me - distance
        wrapped = shard & (N - 1)
        found = jnp.where((entry >> 6) == wrapped, entry_place, 0.0)
        even = jnp.sum(jnp.where(lane < N, found, 0.0), axis=1, keepdims=True)
        odd = jnp.sum(jnp.where(lane < N, 0.0, found), axis=1, keepdims=True)
        sender = sender_of(wrapped, lane_slot)
        hit = (sender >> 1) == pair
        place = jnp.sum(jnp.where(hit, jnp.where((sender & 1) == 0, even, odd), 0.0), axis=0, keepdims=True)
        row = (shard * SHARD).astype(jnp.float32) + place * BLOCK + lane_token
        for g in range(G):
            across = jnp.where(eye, row[:, g * ROWS:(g + 1) * ROWS], 0.0)
            kpos[g, buf * ROWS:(buf + 1) * ROWS, :] = jnp.sum(across, axis=1, keepdims=True)
            if buf == 0:
                qhi[g] = row[:, g * ROWS:(g + 1) * ROWS]
        if buf == 0:
            qplace[...] = row - (shard * SHARD).astype(jnp.float32)
            own_place = place

    my_docs = docs[pl.ds(lax.div(me, 2), 1), :].astype(jnp.float32)
    at = iota((N, 1), 0)
    doc_col = jnp.sum(jnp.where(lane == at + shift, my_docs, 0.0), axis=1, keepdims=True)

    def count(r, total):
        return total + jnp.where(docs[pl.ds(r, 1), :].astype(jnp.float32) < doc_col, 1.0, 0.0)

    counted = lax.fori_loop(0, 32, count, jnp.zeros((N, 128), jnp.float32))
    start_col = jnp.sum(counted, axis=1, keepdims=True) * BLOCK
    low = jnp.sum(jnp.where(own_place == at.astype(jnp.float32), start_col, 0.0), axis=0, keepdims=True)
    for g in range(G):
        qlo[g] = low[:, g * ROWS:(g + 1) * ROWS]

    group_ready(1)
    load_wq.wait()

    @pl.loop(0, G + 3)
    def _(step):
        @pl.when(step < G)
        def _():
            for side in range(2):
                x_send(step, side).wait_recv()
                relay(step, side).start()

        @pl.when((step >= 3) & (step <= G))
        def _():
            pass_on(step - 2)

        @pl.when((step >= 1) & (step <= G))
        def _():
            project(step - 1)

        @pl.when(step + 2 < G)
        def _():
            group_ready(step + 2)

        @pl.when(step == 1)
        def _():
            pass_on(0)

        @pl.when(step == 2)
        def _():
            share(0)

        @pl.when((step == 2) | (step >= 4))
        def _():
            chain_end(jnp.where(step == 2, 0, step - 3))

        j = jnp.where(step <= 3, 0, step - 3)
        there = jnp.minimum(step, G)
        pairs = jnp.where(step < 2, 0, jnp.where(step == 2, 2, jnp.where(step == 3, 1, there + jnp.where(step <= G, j, 0))))

        @pl.loop(0, 3)
        def _(third):
            @pl.when((third == 2) & (step == G))
            def _():
                pass_on(step - 1)

            @pl.when((third == 2) & (step == G + 1))
            def _():
                share(step - 2)

            @pl.loop(lax.div(pairs * third, 3), lax.div(pairs * (third + 1), 3))
            def _(t):
                i = jnp.where(step == 3, 2, jnp.where(t < there, t, there - 1))
                attend(i, jnp.where(t < there, j, t - there))

        @pl.when((step >= 3) & (step <= G))
        def _():
            share(step - 2)

    order = jnp.where(iota((SHARD, 1), 0).astype(jnp.float32) == qplace[...], 1.0, 0.0).astype(jnp.bfloat16)
    for h in range(HEADS):
        columns = slice(h * HEAD_SIZE, (h + 1) * HEAD_SIZE)
        part = jnp.concatenate([o_ref[g, :, columns] / l_ref[g, :, columns] for g in range(G)], axis=1)
        out[:, columns] = lax.dot_general(
            order, part.astype(jnp.bfloat16), (((1,), (1,)), ((), ())), preferred_element_type=jnp.float32
        ).astype(jnp.bfloat16)

    pltpu.make_async_copy(send.at[pl.ds(1, N - 1)], send.at[pl.ds(1, N - 1)], a2a_send).wait()

    @pl.loop(0, G)
    def _(g):
        for side in range(2):
            x_send(g, side).wait_send()
            relay(g, side).wait_send()
        for h in range(3):
            kv_copy(g, h).wait_send()
            pb_copy(g, h).wait_send()


def per_device(tokens, w_query, key_value_weight, bias_query, key_value_bias, destination, doc_ids):
    vmem, hbm = (pl.BlockSpec(memory_space=s) for s in (pltpu.VMEM, pl.ANY))
    bf16, f32 = jnp.bfloat16, jnp.float32
    dma = pltpu.SemaphoreType.DMA
    return pl.pallas_call(
        kernel,
        out_shape=jax.ShapeDtypeStruct((SHARD, QW), bf16),
        in_specs=[vmem, vmem, vmem, vmem, hbm, hbm, hbm],
        out_specs=vmem,
        scratch_shapes=[
            pltpu.VMEM((SHARD, DEPTH), bf16),
            pltpu.VMEM((N, 2 * BLOCK, HALF), bf16),
            pltpu.VMEM((X, N, 2 * BLOCK, HALF), bf16),
            pltpu.VMEM((X * DEPTH, QW), bf16),
            pltpu.VMEM((2 * X * DEPTH, HEAD_SIZE), bf16),
            pltpu.VMEM((X * DEPTH, 2 * HEAD_SIZE), bf16),
            pltpu.VMEM((ROWS, QW + 2 * HEAD_SIZE), f32),
            pltpu.VMEM((G, HEADS * ROWS, HEAD_SIZE), bf16),
            pltpu.VMEM((4, G, ROWS, 2 * HEAD_SIZE), bf16),
            pltpu.VMEM((3, G, ROWS, 2 * HEAD_SIZE), bf16),
            pltpu.VMEM((G, 1, HEADS * ROWS), f32),
            pltpu.VMEM((G, 1, HEADS * ROWS), f32),
            pltpu.VMEM((G, HEAD_SIZE, HEADS * ROWS), f32),
            pltpu.VMEM((512, HEAD_SIZE), f32),
            pltpu.VMEM((G, KEYS, 1), f32),
            pltpu.VMEM((G, 1, ROWS), f32),
            pltpu.VMEM((G, 1, ROWS), f32),
            pltpu.VMEM((1, SHARD), f32),
            dma((3,)), dma, dma((G,)),
            dma((2, G)), dma((2, G)), dma((2, G)), dma((2, G)),
            dma((3, G)), dma((3, G)), dma((3, G)), dma((3, G)),
        ],
        compiler_params=pltpu.CompilerParams(
            collective_id=0, has_side_effects=True, vmem_limit_bytes=56 * 1024 * 1024),
    )(destination.reshape(N // 2, 128), doc_ids.reshape(N // 2, 128), bias_query.reshape(HEADS, HEAD_SIZE), key_value_bias,
      tokens, w_query, key_value_weight.reshape(2 * X * DEPTH, HEAD_SIZE))


def solution(mesh):
    placed = (
        P("ctx", "head"),
        P(None, "head"),
        P(None, None, "head"),
        P("head"),
        P(None, "head"),
        P(),
        P(),
    )
    return jax.shard_map(
        per_device, mesh=mesh, in_specs=placed, out_specs=P("ctx", "head"), check_vma=False
    )
```

```python
import functools
import math

import jax
import jax.numpy as jnp
from jax import lax
from jax.experimental import pallas as pl
from jax.experimental.pallas import tpu as pltpu
from jax.sharding import PartitionSpec as P

MESH = pl.DeviceIdType.MESH
HEAD_SIZE = 128
HEADS = 5
BLOCK = 8
Y, Z, C, X = 4, 8, 2, 4
N = Y * Z * C
G = 4
PER = N // G
ROWS = PER * BLOCK
SHARD = N * BLOCK
HALF = 640
DEPTH = 2 * HALF
QW = HEADS * HEAD_SIZE
DISTANCES = (0, 2, 4, 6, 1, 3, 5)
NBUF = len(DISTANCES)
KEYS = NBUF * ROWS
NEG = -1e30
SCALE = 1.0 / math.sqrt(HEAD_SIZE) * math.log2(math.e)


def slot_parts(slot):
    order = slot >> 3
    dz = (((order + 1) >> 1) * (2 * (order & 1) - 1)) & (Z - 1)
    return (slot >> 1) & (Y - 1), dz, slot & 1


def sender_of(ctx, slot):
    dy, dz, dc = slot_parts(slot)
    return ((((ctx >> 4) - dy) & (Y - 1)) << 4) + ((((ctx >> 1) - dz) & (Z - 1)) << 1) + ((ctx - dc) & 1)


def target_of(ctx, slot):
    dy, dz, dc = slot_parts(slot)
    return ((((ctx >> 4) + dy) & (Y - 1)) << 4) + ((((ctx >> 1) + dz) & (Z - 1)) << 1) + ((ctx + dc) & 1)


def iota(shape, dim):
    return lax.broadcasted_iota(jnp.int32, shape, dim)


def kernel(table, docs, bq, bkv, tokens, wq_hbm, wkv_hbm, out,
           tok, send, xg, wq, wraw, wkv, acc, qs, kv, pb, m_ref, l_ref, o_ref, stage,
           kpos, qlo, qhi, qplace,
           local_sem, a2a_send, a2a_recv, xs_send, x_recv, rl_send, rl_recv,
           kv_send, kv_recv, pb_send, pb_recv):
    me = lax.axis_index("ctx")
    x = lax.axis_index("head")
    core = lax.rem(me, C)
    my_y, my_z = lax.div(me, Z * C), lax.rem(lax.div(me, C), Z)
    right, left = lax.rem(x + 1, X), lax.rem(x + X - 1, X)
    onward = lax.rem(me + C, N)
    onward2 = lax.rem(me + 2 * C, N)
    partner = me + 1 - 2 * core

    load_tok = pltpu.make_async_copy(tokens, tok, local_sem.at[0])
    load_wq = pltpu.make_async_copy(wq_hbm, wq, local_sem.at[1])
    load_wkv = pltpu.make_async_copy(wkv_hbm, wraw, local_sem.at[2])
    load_tok.start()
    load_wkv.start()
    load_wq.start()

    barrier = pltpu.get_barrier_semaphore()

    def chip_at(u):
        order, dy = lax.div(u, Y), lax.rem(u, Y)
        dz = Z + lax.div(order + 1, 2) * (2 * lax.rem(order, 2) - 1)
        return (lax.rem(my_y + dy, Y) * Z + lax.rem(my_z + dz, Z)) * C

    def cores_at(u):
        chip = chip_at(u)
        return (2 * u, chip + core), (2 * u + 1, chip + 1 - core)

    pl.semaphore_signal(barrier, inc=1, device_id=(partner, x), device_id_type=MESH)

    @pl.loop(1, N // 2)
    def _(u):
        for _, target in cores_at(u):
            pl.semaphore_signal(barrier, inc=1, device_id=(target, x), device_id_type=MESH)

    pl.semaphore_signal(barrier, inc=1, device_id=(me, right), device_id_type=MESH)
    pl.semaphore_signal(barrier, inc=1, device_id=(me, left), device_id_type=MESH)

    shift = (me & 1) * N
    mine = table[pl.ds(lax.div(me, 2), 1), :]
    spread = jnp.where(iota((128, SHARD), 0) == shift + (iota((128, SHARD), 1) >> 3), 1.0, 0.0).astype(jnp.bfloat16)
    owners = jnp.broadcast_to((mine >> 6).astype(jnp.float32).astype(jnp.bfloat16), (8, 128))
    owner_of = jnp.dot(owners, spread, preferred_element_type=jnp.float32)[0:1].astype(jnp.int32)
    load_tok.wait()

    def a2a(s, target):
        return pltpu.make_async_remote_copy(
            src_ref=send.at[s], dst_ref=xg.at[0, s], send_sem=a2a_send, recv_sem=a2a_recv.at[lax.div(s, PER)],
            device_id=(target, x), device_id_type=MESH)

    for g in range(G):
        row = iota((ROWS, 1), 0)
        target = target_of(me, (row >> 3) + g * PER)
        pick = (owner_of == target) & ((iota((1, SHARD), 1) & 7) == (row & 7))
        picked = jnp.dot(jnp.where(pick, 1.0, 0.0).astype(jnp.bfloat16), tok[...], preferred_element_type=jnp.float32)
        halves = [picked[:, h * HALF:(h + 1) * HALF].reshape(PER, BLOCK, HALF) for h in range(2)]
        send[pl.ds(g * PER, PER)] = jnp.concatenate(halves, axis=1).astype(jnp.bfloat16)
        if g == 0:
            pl.semaphore_wait(barrier, N + 1)
            pltpu.make_async_copy(send.at[0], xg.at[0, 0], a2a_recv.at[0]).start()
            a2a(1, partner).start()

        @pl.loop(max(1, g * PER // 2), (g + 1) * PER // 2)
        def _(u):
            for s, to in cores_at(u):
                a2a(s, to).start()

    def group(g):
        return pl.ds(g * PER, PER)

    def x_send(g, side):
        return pltpu.make_async_remote_copy(
            src_ref=xg.at[0, group(g)], dst_ref=xg.at[1 + side, group(g)],
            send_sem=xs_send.at[side, g], recv_sem=x_recv.at[side, g],
            device_id=(me, right if side == 0 else left), device_id_type=MESH)

    def relay(g, side):
        half = pl.ds(g * PER + side * (PER // 2), PER // 2)
        return pltpu.make_async_remote_copy(
            src_ref=xg.at[1 + side, half], dst_ref=xg.at[3, half],
            send_sem=rl_send.at[side, g], recv_sem=rl_recv.at[side, g],
            device_id=(me, right if side == 0 else left), device_id_type=MESH)

    def kv_copy(g, h):
        return pltpu.make_async_remote_copy(
            src_ref=kv.at[min(h, 1), g], dst_ref=kv.at[h + 1, g],
            send_sem=kv_send.at[h, g], recv_sem=kv_recv.at[h, g],
            device_id=(onward2 if h == 2 else onward, x), device_id_type=MESH)

    def pb_copy(g, i):
        return pltpu.make_async_remote_copy(
            src_ref=kv.at[i + core, g], dst_ref=pb.at[i, g],
            send_sem=pb_send.at[i, g], recv_sem=pb_recv.at[i, g],
            device_id=(partner, x), device_id_type=MESH)

    def group_ready(g):
        pltpu.make_async_copy(xg.at[0, group(g)], xg.at[0, group(g)], a2a_recv.at[g]).wait()
        x_send(g, 0).start()
        x_send(g, 1).start()

    def pass_on(g):
        kv_copy(g, 0).wait_recv()
        kv_copy(g, 1).start()
        kv_copy(g, 2).start()
        pb_copy(g, 0).start()

    def share(g):
        for h in (1, 2):
            kv_copy(g, h).wait_recv()
            pb_copy(g, h).start()

    def chain_end(g):
        for i in range(3):
            pb_copy(g, i).wait_recv()

    m_ref[...] = jnp.full_like(m_ref, NEG)
    l_ref[...] = jnp.zeros_like(l_ref)
    o_ref[...] = jnp.zeros_like(o_ref)

    def project_part(g, part, peer):
        piece = xg[part, group(g)].astype(jnp.float32)
        lhs = jnp.concatenate(
            [piece[:, :BLOCK].reshape(ROWS, HALF), piece[:, BLOCK:].reshape(ROWS, HALF)], axis=1
        ).astype(jnp.bfloat16)
        depth = pl.ds(pl.multiple_of(peer * DEPTH, DEPTH), DEPTH)
        acc[:, :QW] += jnp.dot(lhs, wq[depth, :], preferred_element_type=jnp.float32)
        acc[:, QW:] += jnp.dot(lhs, wkv[depth, :], preferred_element_type=jnp.float32)

    def project(g):
        acc[...] = jnp.concatenate(
            [jnp.broadcast_to(b[h:h + 1, :], (ROWS, HEAD_SIZE)) for b in (bq, bkv) for h in range(b.shape[0])], axis=1)

        @pl.loop(0, 4)
        def _(part):
            @pl.when(part == 3)
            def _():
                relay(g, 0).wait_recv()
                relay(g, 1).wait_recv()

            shift = jnp.where(part == 3, 2, jnp.where(part == 1, X - 1, jnp.where(part == 2, 1, 0)))
            project_part(g, part, lax.rem(x + shift, X))

        for h in range(HEADS):
            qs[g, pl.ds(h * ROWS, ROWS), :] = acc[:, h * HEAD_SIZE:(h + 1) * HEAD_SIZE].astype(jnp.bfloat16)
        kv[0, g] = jnp.concatenate(
            [acc[:, QW:QW + HEAD_SIZE], acc[:, QW + HEAD_SIZE:].T], axis=1).astype(jnp.bfloat16)
        kv_copy(g, 0).start()

    def attend(i, j):
        blocks = [kv[h, j] for h in range(4)] + [pb[h, j] for h in range(3)]
        keys = jnp.concatenate([block[:, :HEAD_SIZE] for block in blocks], axis=0)
        values = jnp.concatenate([block[:, HEAD_SIZE:] for block in blocks], axis=1)
        values = jnp.concatenate([values, jnp.ones((16, KEYS), jnp.bfloat16)], axis=0)
        place = kpos[j]
        bias = jnp.where((place <= qhi[i]) & (place >= qlo[i]), 0.0, NEG)
        s = lax.dot_general(keys, qs[i], (((1,), (1,)), ((), ())), preferred_element_type=jnp.float32)
        s = s + jnp.concatenate([bias] * HEADS, axis=1)
        m_old = m_ref[i]
        m_new = jnp.maximum(m_old, jnp.max(s, axis=0, keepdims=True))
        p = jnp.exp2((s - m_new) * SCALE).astype(jnp.bfloat16)
        alpha = jnp.exp2((m_old - m_new) * SCALE)
        added = jnp.dot(values, p, preferred_element_type=jnp.float32)
        o_ref[i] = o_ref[i] * alpha + added[:HEAD_SIZE]
        l_ref[i] = l_ref[i] * alpha + added[HEAD_SIZE:HEAD_SIZE + 1]
        m_ref[i] = m_new

    group_ready(0)

    load_wkv.wait()

    @pl.loop(0, 20)
    def _(t):
        raw = wraw[pl.ds(t * 512, 512), :].astype(jnp.float32)
        stage[...] = raw
        rows = pl.ds(t * 256, 256)
        wkv[rows, :HEAD_SIZE] = stage[pl.ds(0, 256, 2), :].astype(jnp.bfloat16)
        wkv[rows, HEAD_SIZE:] = stage[pl.ds(1, 256, 2), :].astype(jnp.bfloat16)

    entry = table[...]
    entry_place = (entry & (N - 1)).astype(jnp.float32)
    lane = iota((1, 128), 1)
    lane_slot = iota((1, SHARD), 1) >> 3
    lane_token = (iota((1, SHARD), 1) & 7).astype(jnp.float32)
    pair = iota((N // 2, 1), 0)
    eye = iota((ROWS, ROWS), 0) == iota((ROWS, ROWS), 1)
    for buf, distance in enumerate(DISTANCES):
        shard = me - distance
        wrapped = shard & (N - 1)
        found = jnp.where((entry >> 6) == wrapped, entry_place, 0.0)
        even = jnp.sum(jnp.where(lane < N, found, 0.0), axis=1, keepdims=True)
        odd = jnp.sum(jnp.where(lane < N, 0.0, found), axis=1, keepdims=True)
        sender = sender_of(wrapped, lane_slot)
        hit = (sender >> 1) == pair
        place = jnp.sum(jnp.where(hit, jnp.where((sender & 1) == 0, even, odd), 0.0), axis=0, keepdims=True)
        row = (shard * SHARD).astype(jnp.float32) + place * BLOCK + lane_token
        for g in range(G):
            across = jnp.where(eye, row[:, g * ROWS:(g + 1) * ROWS], 0.0)
            kpos[g, buf * ROWS:(buf + 1) * ROWS, :] = jnp.sum(across, axis=1, keepdims=True)
            if buf == 0:
                qhi[g] = row[:, g * ROWS:(g + 1) * ROWS]
        if buf == 0:
            qplace[...] = row - (shard * SHARD).astype(jnp.float32)
            own_place = place

    my_docs = docs[pl.ds(lax.div(me, 2), 1), :].astype(jnp.float32)
    at = iota((N, 1), 0)
    doc_col = jnp.sum(jnp.where(lane == at + shift, my_docs, 0.0), axis=1, keepdims=True)

    def count(r, total):
        return total + jnp.where(docs[pl.ds(r, 1), :].astype(jnp.float32) < doc_col, 1.0, 0.0)

    counted = lax.fori_loop(0, 32, count, jnp.zeros((N, 128), jnp.float32))
    start_col = jnp.sum(counted, axis=1, keepdims=True) * BLOCK
    low = jnp.sum(jnp.where(own_place == at.astype(jnp.float32), start_col, 0.0), axis=0, keepdims=True)
    for g in range(G):
        qlo[g] = low[:, g * ROWS:(g + 1) * ROWS]

    group_ready(1)
    load_wq.wait()

    @pl.loop(0, G + 3)
    def _(step):
        @pl.when(step < G)
        def _():
            for side in range(2):
                x_send(step, side).wait_recv()
                relay(step, side).start()

        @pl.when((step >= 3) & (step <= G))
        def _():
            pass_on(step - 2)

        @pl.when((step >= 1) & (step <= G))
        def _():
            project(step - 1)

        @pl.when(step + 2 < G)
        def _():
            group_ready(step + 2)

        @pl.when(step == 1)
        def _():
            pass_on(0)

        @pl.when(step == 2)
        def _():
            share(0)

        @pl.when((step == 2) | (step >= 4))
        def _():
            chain_end(jnp.where(step == 2, 0, step - 3))

        j = jnp.where(step <= 3, 0, step - 3)
        there = jnp.minimum(step, G)
        pairs = jnp.where(step < 2, 0, jnp.where(step == 2, 2, jnp.where(step == 3, 1, there + jnp.where(step <= G, j, 0))))

        @pl.loop(0, 3)
        def _(third):
            @pl.when((third == 2) & (step == G))
            def _():
                share(step - 2)
                pass_on(step - 1)

            @pl.when((third == 2) & (step == G + 1))
            def _():
                share(step - 2)

            @pl.loop(lax.div(pairs * third, 3), lax.div(pairs * (third + 1), 3))
            def _(t):
                i = jnp.where(step == 3, 2, jnp.where(t < there, t, there - 1))
                attend(i, jnp.where(t < there, j, t - there))

        @pl.when(step == 3)
        def _():
            share(step - 2)

    order = jnp.where(iota((SHARD, 1), 0).astype(jnp.float32) == qplace[...], 1.0, 0.0).astype(jnp.bfloat16)
    for h in range(HEADS):
        columns = slice(h * HEAD_SIZE, (h + 1) * HEAD_SIZE)
        part = jnp.concatenate([o_ref[g, :, columns] / l_ref[g, :, columns] for g in range(G)], axis=1)
        out[:, columns] = lax.dot_general(
            order, part.astype(jnp.bfloat16), (((1,), (1,)), ((), ())), preferred_element_type=jnp.float32
        ).astype(jnp.bfloat16)

    pltpu.make_async_copy(send.at[pl.ds(1, N - 1)], send.at[pl.ds(1, N - 1)], a2a_send).wait()

    @pl.loop(0, G)
    def _(g):
        for side in range(2):
            x_send(g, side).wait_send()
            relay(g, side).wait_send()
        for h in range(3):
            kv_copy(g, h).wait_send()
            pb_copy(g, h).wait_send()


def per_device(tokens, w_query, key_value_weight, bias_query, key_value_bias, destination, doc_ids):
    vmem, hbm = (pl.BlockSpec(memory_space=s) for s in (pltpu.VMEM, pl.ANY))
    bf16, f32 = jnp.bfloat16, jnp.float32
    dma = pltpu.SemaphoreType.DMA
    return pl.pallas_call(
        kernel,
        out_shape=jax.ShapeDtypeStruct((SHARD, QW), bf16),
        in_specs=[vmem, vmem, vmem, vmem, hbm, hbm, hbm],
        out_specs=vmem,
        scratch_shapes=[
            pltpu.VMEM((SHARD, DEPTH), bf16),
            pltpu.VMEM((N, 2 * BLOCK, HALF), bf16),
            pltpu.VMEM((X, N, 2 * BLOCK, HALF), bf16),
            pltpu.VMEM((X * DEPTH, QW), bf16),
            pltpu.VMEM((2 * X * DEPTH, HEAD_SIZE), bf16),
            pltpu.VMEM((X * DEPTH, 2 * HEAD_SIZE), bf16),
            pltpu.VMEM((ROWS, QW + 2 * HEAD_SIZE), f32),
            pltpu.VMEM((G, HEADS * ROWS, HEAD_SIZE), bf16),
            pltpu.VMEM((4, G, ROWS, 2 * HEAD_SIZE), bf16),
            pltpu.VMEM((3, G, ROWS, 2 * HEAD_SIZE), bf16),
            pltpu.VMEM((G, 1, HEADS * ROWS), f32),
            pltpu.VMEM((G, 1, HEADS * ROWS), f32),
            pltpu.VMEM((G, HEAD_SIZE, HEADS * ROWS), f32),
            pltpu.VMEM((512, HEAD_SIZE), f32),
            pltpu.VMEM((G, KEYS, 1), f32),
            pltpu.VMEM((G, 1, ROWS), f32),
            pltpu.VMEM((G, 1, ROWS), f32),
            pltpu.VMEM((1, SHARD), f32),
            dma((3,)), dma, dma((G,)),
            dma((2, G)), dma((2, G)), dma((2, G)), dma((2, G)),
            dma((3, G)), dma((3, G)), dma((3, G)), dma((3, G)),
        ],
        compiler_params=pltpu.CompilerParams(
            collective_id=0, has_side_effects=True, vmem_limit_bytes=56 * 1024 * 1024),
    )(destination.reshape(N // 2, 128), doc_ids.reshape(N // 2, 128), bias_query.reshape(HEADS, HEAD_SIZE), key_value_bias,
      tokens, w_query, key_value_weight.reshape(2 * X * DEPTH, HEAD_SIZE))


def solution(mesh):
    placed = (
        P("ctx", "head"),
        P(None, "head"),
        P(None, None, "head"),
        P("head"),
        P(None, "head"),
        P(),
        P(),
    )
    return jax.shard_map(
        per_device, mesh=mesh, in_specs=placed, out_specs=P("ctx", "head"), check_vma=False
    )
```
